1024 devices in a mesh: dom: 128 (over x, y, core), band: 8 (over z).
Axes of the slice: x: 8, y: 8, z: 8, core: 2. Of those that a mesh axis runs over, the one named last changes fastest.
Arguments:
- orbitals: float32 [16, 128, 4096], P('band', 'dom'), may hold values from -18 to 18
- potential: float32 [128, 4096], P('dom'), may hold values from -2 to 0
- support: int32 [65536], P('dom'), may hold values from 0 to 4095, as said below
- proj: float32 [16, 65536], P(None, 'dom'), may hold values from -0.125 to 0.125
- offsets: int32 [128], replicated, may hold values from 0 to 1023, as said below
- coupling: float32 [1024], replicated, may hold values from 0.2 to 1
Outputs:
- rotated: float32 [16, 128, 4096], P('band', 'dom')
- projected: float32 [16, 16], replicated
The draws below stay inside these ranges and needn't reach their ends.
Inputs may be any that keep to these rules, and one draw needn't show every extreme that they name: `support`: on each domain the 512 entries are strictly increasing local cell indices; the first is 0 and the last is 4095. offsets[d] lies in [8 d, 8 (d + 1)).
All inputs are finite; a program needn't handle non-finite values.
Results may differ from the reference program's by a relative error of at most 0.0003.
Values sent between devices are 32-bit elements; how exact they have to be, the bound alone decides.
A program may use at most 32 MiB of HBM per device.

```python
import math
import jax
import jax.numpy as jnp
from jax import lax

BX = 8
BY = 16
BZ = 32
SUPP = 512
ORB = 16
DEG = 4
NS_ITERS = 10
PSTR = 8
PBLK = 16
NPROJ = 1024
DZ = 4
DY = 4
DX = 8
CELLS = 4096
NX = 64
NY = 64
NZ = 128
N_DOM = 128


def draw_orbitals(key, part):
    key = jax.random.fold_in(key, 5)
    keys = jax.random.split(key, 4)
    shape = (ORB, N_DOM, CELLS)
    own = jax.random.truncated_normal(keys[0], -3.0, 3.0, shape, jnp.float32)
    mixing = jax.random.uniform(keys[2], (ORB, 4), jnp.float32, -1.2, 1.2)
    common = jax.random.truncated_normal(keys[3], -3.0, 3.0, (4, N_DOM, CELLS), jnp.float32)
    field = own
    for index in range(4):
        field = field + mixing[:, index][:, None, None] * common[index][None]
    return field


def draw_support(key, part):
    key = jax.random.fold_in(key, 11)
    stride = CELLS // SUPP
    starts = jnp.arange(SUPP, dtype=jnp.int32) * stride
    jitter = jax.random.randint(key, (N_DOM, SUPP), 0, stride, dtype=jnp.int32)
    chosen = starts[None, :] + jitter
    chosen = chosen.at[:, 0].set(0).at[:, SUPP - 1].set(CELLS - 1)
    return chosen.reshape(N_DOM * SUPP)


def draw_offsets(key, part):
    key = jax.random.fold_in(key, 23)
    jitter = jax.random.randint(key, (N_DOM,), 0, PSTR, dtype=jnp.int32)
    jitter = jitter.at[0].set(0).at[N_DOM - 1].set(PSTR - 1)
    return jnp.arange(N_DOM, dtype=jnp.int32) * PSTR + jitter


def block_scale(own_key, dims, cuts, least, high):
    gain = 1.0
    for dim, parts in cuts:
        steps = jax.random.uniform(jax.random.fold_in(jax.random.fold_in(own_key, 6), dim), (parts,), jnp.float32, least / len(cuts), high / len(cuts))
        gain = gain * jnp.repeat(jnp.exp(steps), dims[dim] // parts).reshape((-1,) + (1,) * (len(dims) - 1 - dim))
    return gain


def gaussian(key, shape, deviation, most, pieces=(), kind=jnp.bfloat16):
    loudness = block_scale(key, shape, pieces, -0.22, 0.18) if pieces else 1.0
    array = jax.random.normal(key, shape, jnp.float32) * deviation * loudness
    return jnp.minimum(jnp.maximum(array, -most), most).astype(kind)


def setup_inputs(seed: int = 0) -> dict:
    key_of = jax.random.split(jax.random.key(seed), 7)
    orbitals = draw_orbitals(jax.random.fold_in(key_of[6], 71), 0)
    potential = jnp.clip(-2.0 + 2.0 * jax.random.uniform(key_of[1], (N_DOM, CELLS), jnp.float32) ** block_scale(key_of[1], (N_DOM, CELLS), ((0, 128),), -0.2, 0.2), -2.0, 0.0)
    support = draw_support(jax.random.fold_in(key_of[6], 71), 0)
    proj = gaussian(key_of[3], (PBLK, N_DOM * SUPP), (4 * SUPP) ** -0.5, 0.125, ((1, 128),), jnp.float32)
    offsets = draw_offsets(jax.random.fold_in(key_of[6], 71), 0)
    coupling = jnp.clip(jnp.exp(jax.random.uniform(key_of[5], (NPROJ,), jnp.float32, math.log(0.2), math.log(1.0))), 0.2, 1.0)
    return dict(orbitals=orbitals, potential=potential, support=support, proj=proj, offsets=offsets, coupling=coupling)


STENCIL = [-5369.0 / 1800.0, 12.0 / 7.0, -15.0 / 56.0, 10.0 / 189.0, -1.0 / 112.0, 2.0 / 1925.0, -1.0 / 16632.0]
CENTER = 10.0
HALF_WIDTH = 6.0

def inverse_root(correlation):
    order = correlation.shape[0]
    norm_scale = jnp.sqrt(jnp.sum(correlation * correlation))
    iterate = correlation / norm_scale
    inverse = jnp.eye(order, dtype=jnp.float32)
    identity = jnp.eye(order, dtype=jnp.float32)
    for sweep in range(NS_ITERS):
        middle = 1.5 * identity - 0.5 * jnp.dot(inverse, iterate, precision=lax.Precision.HIGHEST)
        iterate = jnp.dot(iterate, middle, precision=lax.Precision.HIGHEST)
        inverse = jnp.dot(middle, inverse, precision=lax.Precision.HIGHEST)
    return inverse / jnp.sqrt(norm_scale)

def to_grid(blocked):
    return blocked.reshape(DX, DY, DZ, BX, BY, BZ).transpose(0, 3, 1, 4, 2, 5).reshape(NX, NY, NZ)

def to_blocks(grid_field):
    return grid_field.reshape(DX, BX, DY, BY, DZ, BZ).transpose(0, 2, 4, 1, 3, 5).reshape(N_DOM, CELLS)

def reference(orbitals, potential, support, proj, offsets, coupling):
    rows = jnp.arange(N_DOM, dtype=jnp.int32)[:, None] * CELLS
    global_cells = (rows + support.reshape(N_DOM, SUPP).astype(jnp.int32)).reshape(-1)
    proj_three = proj.reshape(PBLK, N_DOM, SUPP)
    proj_ids = (offsets[:, None] + jnp.arange(PBLK, dtype=jnp.int32)[None, :]) % NPROJ
    flat_ids = proj_ids.reshape(-1)

    def apply_one(blocked_field):
        grid_field = to_grid(blocked_field)
        laplace = 3.0 * STENCIL[0] * grid_field
        for reach in range(1, 7):
            beside_all = jnp.zeros_like(grid_field)
            for axis_id in range(3):
                beside_all = beside_all + jnp.roll(grid_field, reach, axis_id) + jnp.roll(grid_field, -reach, axis_id)
            laplace = laplace + STENCIL[reach] * beside_all
        flat_field = blocked_field.reshape(-1)
        picked = flat_field[global_cells].reshape(N_DOM, SUPP)
        inner_prod = jnp.einsum('ds,pds->dp', picked, proj_three, precision=lax.Precision.HIGHEST)
        totals = jnp.zeros((NPROJ,), jnp.float32).at[flat_ids].add(inner_prod.reshape(-1))
        own_coeffs = totals[proj_ids] * coupling[proj_ids]
        spread_back = jnp.einsum('dp,pds->ds', own_coeffs, proj_three, precision=lax.Precision.HIGHEST)
        nonlocal_part = jnp.zeros_like(flat_field).at[global_cells].add(spread_back.reshape(-1))
        return -0.5 * to_blocks(laplace) + potential * blocked_field + nonlocal_part.reshape(blocked_field.shape)

    def apply_ham(orbital_block):
        return lax.map(apply_one, orbital_block)
    previous = orbitals
    current = (apply_ham(orbitals) - CENTER * orbitals) / HALF_WIDTH
    for degree in range(1, DEG):
        following = 2.0 * (apply_ham(current) - CENTER * current) / HALF_WIDTH - previous
        previous = current
        current = following
    filtered = current
    hfield = apply_ham(filtered)
    filtered_flat = filtered.reshape(ORB, -1)
    hfield_flat = hfield.reshape(ORB, -1)
    correlation = jnp.dot(filtered_flat, filtered_flat.T, precision=lax.Precision.HIGHEST)
    hmat = jnp.dot(filtered_flat, hfield_flat.T, precision=lax.Precision.HIGHEST)
    coeffs = inverse_root(correlation)
    projected = jnp.dot(jnp.dot(coeffs.T, hmat, precision=lax.Precision.HIGHEST), coeffs, precision=lax.Precision.HIGHEST)
    rotated = jnp.dot(coeffs.T, filtered_flat, precision=lax.Precision.HIGHEST).reshape(orbitals.shape)
    return (rotated, projected)
```

```python
import functools

import jax
import jax.numpy as jnp
from jax import lax
from jax.experimental import pallas as pl
from jax.experimental.pallas import tpu as pltpu
from jax.sharding import PartitionSpec as P

DEG = 4
ROUNDS = DEG + 1
NS_ITERS = 10
NPROJ = 1024
PBLK = 16
SUPP = 512
DOMS = 128
BANDS = 8

STENCIL = [
    -5369.0 / 1800.0,
    12.0 / 7.0,
    -15.0 / 56.0,
    10.0 / 189.0,
    -1.0 / 112.0,
    2.0 / 1925.0,
    -1.0 / 16632.0,
]
HALF = [-0.5 * c for c in STENCIL]
CENTER = 10.0
HALF_WIDTH = 6.0
F32 = jnp.float32
BF16 = jnp.bfloat16
NT = (((1,), (1,)), ((), ()))


def roll(v, shift, axis):
    return pltpu.roll(v, shift % v.shape[axis], axis)


def iota(shape, axis):
    return lax.broadcasted_iota(jnp.int32, shape, axis)


def split3(v):
    high = v.astype(BF16)
    rest = v - high.astype(F32)
    mid = rest.astype(BF16)
    low = (rest - mid.astype(F32)).astype(BF16)
    return high, mid, low


def dot32(a, b):
    return jnp.dot(a, b, precision=lax.Precision.HIGHEST, preferred_element_type=F32)


def lane_z(shape):
    return iota(shape, len(shape) - 1) % 32


def lane_y(shape):
    return iota(shape, len(shape) - 1) // 32


def row_y(shape):
    return iota(shape, len(shape) - 2) % 4


def pack_y(v):
    pairs = v.reshape(4, 2, 8, 128)
    even, odd = pairs[:, 0], pairs[:, 1]
    yhi = row_y(even.shape)
    swapped = roll(even, 4, 1)
    first = jnp.where(yhi < 2, swapped, roll(odd, 6, 1))
    last = jnp.where(yhi >= 2, swapped, roll(odd, 2, 1))
    return first, last


def unpack_y(first, last):
    below = jnp.stack([last, roll(last, 2, 1)], axis=1).reshape(8, 8, 128)
    above = jnp.stack([first, roll(first, 6, 1)], axis=1).reshape(8, 8, 128)
    return below, above


def pack_z(v):
    quads = v.reshape(2, 4, 8, 128)
    z = lane_z((2, 8, 128))
    first, last = quads[:, 0], roll(quads[:, 0], 104, 2)
    for i in range(1, 4):
        inside = (z >= 8 * i) & (z < 8 * i + 8)
        first = jnp.where(inside, roll(quads[:, i], 8 * i, 2), first)
        last = jnp.where(inside, roll(quads[:, i], 104 + 8 * i, 2), last)
    return first, last


def unpack_z(first, last):
    above = jnp.stack([roll(first, 32 - 8 * i, 2) for i in range(4)], axis=1)
    below = jnp.stack([roll(last, 120 - 8 * i, 2) for i in range(4)], axis=1)
    return below.reshape(8, 8, 128), above.reshape(8, 8, 128)


def sum_x(v, below, above):
    ext = jnp.concatenate([below, v, above], axis=0)
    total = HALF[1] * (ext[7:15] + ext[5:13])
    for k in range(2, 7):
        total = total + HALF[k] * (ext[6 + k : 14 + k] + ext[6 - k : 14 - k])
    return total


def sum_y(v, below, above):
    yhi = row_y(v.shape)
    up1 = roll(jnp.where(yhi < 1, above, v), 7, 1)
    up2 = roll(jnp.where(yhi < 2, above, v), 6, 1)
    dn1 = roll(jnp.where(yhi >= 3, below, v), 1, 1)
    dn2 = roll(jnp.where(yhi >= 2, below, v), 2, 1)
    p = lane_y((1, 8, 128))
    h = HALF

    def pick(edge, upper, lower):
        return jnp.where(p >= edge, jnp.float32(upper), jnp.float32(lower))

    one = (
        pick(1, h[1], h[3]) * v
        + pick(1, h[5], h[1]) * up1
        + pick(1, 0.0, h[5]) * up2
        + pick(1, h[3], 0.0) * dn1
    )
    two = (
        h[2] * v
        + pick(2, h[6], h[2]) * up1
        + pick(2, 0.0, h[6]) * up2
        + pick(2, h[2], h[6]) * dn1
        + pick(2, h[6], 0.0) * dn2
    )
    three = (
        pick(3, h[3], h[1]) * v
        + pick(3, 0.0, h[3]) * up1
        + pick(3, h[1], h[5]) * dn1
        + pick(3, h[5], 0.0) * dn2
    )
    return h[4] * (up1 + dn1) + roll(one, 96, 2) + roll(two, 64, 2) + roll(three, 32, 2)


def sum_z(v, below, above):
    z = lane_z(v.shape)
    total = None
    for k in range(1, 7):
        up = roll(jnp.where(z < k, above, v), 128 - k, 2)
        down = roll(jnp.where(z >= 32 - k, below, v), k, 2)
        term = HALF[k] * (up + down)
        total = term if total is None else total + term
    return total


def spread_projectors(support, proj):
    high_bits = support // 128
    low_bits = support % 128
    rows = (iota((32, SUPP), 0) == high_bits).astype(F32)
    lanes = (iota((128, SUPP), 0) == low_bits).astype(F32).astype(BF16)
    dense = None
    for part in split3(proj):
        left = (part.astype(F32)[:, None, :] * rows[None]).reshape(PBLK * 32, SUPP)
        term = lax.dot_general(left.astype(BF16), lanes, NT, preferred_element_type=F32)
        dense = term if dense is None else dense + term
    dense = dense.reshape(PBLK * 4, 8, 128)
    turned = roll(dense, 4, 1)
    upper = iota(dense.shape, 1) < 4
    even = jnp.where(upper, dense, turned)
    odd = jnp.where(upper, turned, dense)
    return jnp.stack([even, odd], axis=1).reshape(PBLK, 8, 8, 128)


def flatten16(c):
    rep = jnp.concatenate([c] * 8, axis=1)
    own = iota((16, 128), 1) // 16 == iota((16, 128), 0) % 8
    rep = jnp.where(own, rep, 0.0)
    return jnp.sum(rep.reshape(2, 8, 128), axis=1)


def unflatten16(s):
    wide = jnp.concatenate(
        [jnp.broadcast_to(s[0:1], (8, 128)), jnp.broadcast_to(s[1:2], (8, 128))], axis=0
    )
    own = iota((16, 128), 1) // 16 == iota((16, 128), 0) % 8
    wide = jnp.where(own, wide, 0.0)
    for step in (16, 32, 64):
        wide = wide + roll(wide, step, 1)
    return wide


def kernel(
    orb, pot, sup, proj, off, coup, rot_out, prj_out,
    ys, pdense, match, yfirst, ylast, zfirst, zlast,
    xbelow, xabove, ybelow, yabove, zbelow, zabove, inner, hf,
    fslice, hslice, gathered, cz, cx, cy, hz, hx, hy,
    halo_send, halo_recv, inner_send, inner_recv,
    fs_send, fs_recv, hs_send, hs_recv, g_send, g_recv,
    cz_send, cz_recv, cx_send, cx_recv, cy_send, cy_recv,
    hz_send, hz_recv, hx_send, hx_recv, hy_send, hy_recv,
):
    me = lax.axis_index("dom")
    band = lax.axis_index("band")
    ax, ay = me // 16, me % 16
    by, cz_pos = (me // 4) % 4, me % 4

    def dom_x(i):
        return ((ax + i) % 8) * 16 + ay

    def dom_y(i):
        return ax * 16 + (ay + i) % 16

    x_up, x_down = dom_x(1), dom_x(7)
    y_up = ax * 16 + ((by + 1) % 4) * 4 + cz_pos
    y_down = ax * 16 + ((by + 3) % 4) * 4 + cz_pos
    z_up = me - cz_pos + (cz_pos + 1) % 4
    z_down = me - cz_pos + (cz_pos + 3) % 4
    chain = [((me + step) % DOMS, 2 - step) for step in (-2 + DOMS, -1 + DOMS, 1, 2)]
    chain = [(dom, slot + DOMS if slot < 0 else slot) for dom, slot in chain]

    barrier = pltpu.get_barrier_semaphore()
    greeted = [(dom_x(i), band) for i in range(1, 8)]
    greeted += [(dom_y(i), band) for i in range(1, 16)]
    greeted += [(me, (band + i) % BANDS) for i in range(1, 8)]
    greeted += [(dom, band) for dom, _ in chain]
    for device in greeted:
        pl.semaphore_signal(barrier, inc=1, device_id=device, device_id_type=pl.DeviceIdType.MESH)

    started = []

    def send(src, dst, ssem, rsem, dom, to_band):
        copy = pltpu.make_async_remote_copy(
            src_ref=src, dst_ref=dst, send_sem=ssem, recv_sem=rsem,
            device_id=(dom, to_band), device_id_type=pl.DeviceIdType.MESH,
        )
        copy.start()
        started.append(copy)

    def await_copy(src, dst, ssem, rsem):
        pltpu.make_async_remote_copy(
            src_ref=src, dst_ref=dst, send_sem=ssem, recv_sem=rsem,
            device_id=(me, band), device_id_type=pl.DeviceIdType.MESH,
        ).wait_recv()

    def share(buf, ssem, rsem, pos, count, place):
        for i in range(1, count):
            dom, to_band = place(i)
            send(buf.at[pos], buf.at[pos], ssem.at[i], rsem.at[pos], dom, to_band)

    def await_shares(buf, ssem, rsem, pos, count):
        for i in range(1, count):
            source = (pos + count - i) % count
            await_copy(buf.at[source], buf.at[source], ssem.at[i], rsem.at[source])

    def place_z(i):
        return me, (band + i) % BANDS

    def place_x(i):
        return dom_x(i), band

    def place_y(i):
        return dom_y(i), band

    def send_halos(k, v):
        y_first, y_last = pack_y(v)
        z_first, z_last = pack_z(v)
        yfirst[k], ylast[k] = y_first, y_last
        zfirst[k], zlast[k] = z_first, z_last
        block = ys.at[k]
        hs, hr = halo_send.at[k], halo_recv.at[k]
        send(yfirst.at[k], yabove.at[k], hs.at[0], hr.at[0], y_down, band)
        send(ylast.at[k], ybelow.at[k], hs.at[1], hr.at[1], y_up, band)
        send(block.at[pl.ds(0, 6)], xabove.at[k], hs.at[2], hr.at[2], x_down, band)
        send(block.at[pl.ds(2, 6)], xbelow.at[k], hs.at[3], hr.at[3], x_up, band)
        send(zfirst.at[k], zabove.at[k], hs.at[4], hr.at[4], z_down, band)
        send(zlast.at[k], zbelow.at[k], hs.at[5], hr.at[5], z_up, band)

    def send_inner(k, v):
        sums = jnp.concatenate([jnp.sum(pdense[j] * v, axis=0) for j in range(PBLK)], axis=0)
        ones = jnp.ones((8, 384), BF16)
        parts = jnp.concatenate(split3(sums), axis=1)
        flat = lax.dot_general(ones, parts, NT, preferred_element_type=F32)
        inner[k, 2] = flat[0:1]
        for i, (dom, slot) in enumerate(chain):
            send(inner.at[k, 2], inner.at[k, slot], inner_send.at[k, i], inner_recv.at[k, slot], dom, band)

    def apply_h(k, v, own, couple):
        hs, hr = halo_send.at[k], halo_recv.at[k]
        await_copy(zabove.at[k], zabove.at[k], hs.at[4], hr.at[4])
        await_copy(zbelow.at[k], zbelow.at[k], hs.at[5], hr.at[5])
        field = own * v + sum_z(v, *unpack_z(zabove[k], zbelow[k]))
        await_copy(xabove.at[k], xabove.at[k], hs.at[2], hr.at[2])
        await_copy(xbelow.at[k], xbelow.at[k], hs.at[3], hr.at[3])
        field = field + sum_x(v, xbelow[k], xabove[k])
        await_copy(yabove.at[k], yabove.at[k], hs.at[0], hr.at[0])
        await_copy(ybelow.at[k], ybelow.at[k], hs.at[1], hr.at[1])
        field = field + sum_y(v, *unpack_y(yabove[k], ybelow[k]))
        for i, (_, slot) in enumerate(chain):
            slot = 4 - slot
            await_copy(inner.at[k, slot], inner.at[k, slot], inner_send.at[k, i], inner_recv.at[k, slot])
        rows = jnp.concatenate([inner[k, slot] for slot in range(5)], axis=1)
        mine = (iota((8, 640), 1) // 4) % 2 == iota((8, 640), 0) // 4
        rows = jnp.where(mine, jnp.broadcast_to(rows, (8, 640)), 0.0)
        parts = [part.astype(F32) for part in split3(rows)]
        stacked = jnp.concatenate(parts + [jnp.zeros((8, 640), F32)], axis=0).astype(BF16)
        totals = jnp.dot(stacked, match[...], preferred_element_type=F32)
        coefs = (totals[0:8] + totals[8:16] + totals[16:24]) * couple
        for j in range(PBLK):
            field = field + jnp.broadcast_to(coefs[:, j : j + 1], (8, 128))[None] * pdense[j]
        return field

    ys[0, :, 0:4, :] = orb[0]
    ys[0, :, 4:8, :] = orb[1]
    current = ys[0]
    pots = jnp.concatenate([pot[...], pot[...]], axis=1)
    own = pots + jnp.float32(3.0 * HALF[0])
    pl.semaphore_wait(barrier, len(greeted))
    send_halos(0, current)
    pdense[...] = spread_projectors(sup[...], proj[...])
    send_inner(0, current)
    first_id = off[me]
    couple = jnp.zeros((1, 128), F32)
    lane = iota((1, 128), 1)
    for j in range(PBLK):
        couple = jnp.where(lane == j, coup[(first_id + j) % NPROJ], couple)
    wanted = (first_id + iota((128, 128), 1)) % NPROJ
    for slot in range(5):
        theirs = off[(me + slot - 2 + DOMS) % DOMS]
        have = (theirs + iota((128, 128), 0) // 8) % NPROJ
        match[slot * 128 : slot * 128 + 128, :] = jnp.where(have == wanted, 1.0, 0.0).astype(BF16)

    previous = current
    current = (apply_h(0, current, own, couple) - CENTER * current) * (1.0 / HALF_WIDTH)
    for k in range(1, DEG):
        ys[k] = current
        send_halos(k, current)
        send_inner(k, current)
        following = (apply_h(k, current, own, couple) - CENTER * current) * (2.0 / HALF_WIDTH) - previous
        previous, current = current, following
    ys[DEG] = current

    def spread_layers(block, buf, ssem, rsem):
        for i in range(1, BANDS):
            to = (band + i) % BANDS
            send(block.at[to], buf.at[band], ssem.at[i], rsem.at[band], me, to)
        buf[band] = block[band]

    def layer_rows(buf):
        flat = buf.reshape(64, 128)
        return jnp.concatenate([flat[pl.ds(y, 16, stride=4), :] for y in range(4)], axis=1)

    def product(a, b):
        return lax.dot_general(a, b, NT, precision=lax.Precision.HIGHEST, preferred_element_type=F32)

    spread_layers(ys.at[DEG], fslice, fs_send, fs_recv)
    send_halos(DEG, current)
    send_inner(DEG, current)
    await_shares(fslice, fs_send, fs_recv, band, BANDS)
    layer = layer_rows(fslice)
    cz[band] = flatten16(product(layer, layer))
    share(cz, cz_send, cz_recv, band, BANDS, place_z)
    hfield = apply_h(DEG, current, own, couple)
    hf[...] = hfield
    spread_layers(hf, hslice, hs_send, hs_recv)
    await_shares(cz, cz_send, cz_recv, band, BANDS)
    cx[ax] = jnp.sum(cz[...], axis=0)
    share(cx, cx_send, cx_recv, ax, 8, place_x)
    await_shares(hslice, hs_send, hs_recv, band, BANDS)
    hz[band] = flatten16(product(layer, layer_rows(hslice)))
    share(hz, hz_send, hz_recv, band, BANDS, place_z)
    for i in range(1, BANDS):
        send(ys.at[DEG], gathered.at[band], g_send.at[i], g_recv.at[band], *place_z(i))
    gathered[band] = current
    await_shares(cx, cx_send, cx_recv, ax, 8)
    cy[ay] = jnp.sum(cx[...], axis=0)
    share(cy, cy_send, cy_recv, ay, 16, place_y)
    await_shares(hz, hz_send, hz_recv, band, BANDS)
    hx[ax] = jnp.sum(hz[...], axis=0)
    share(hx, hx_send, hx_recv, ax, 8, place_x)
    await_shares(cy, cy_send, cy_recv, ay, 16)
    corr = jnp.sum(cy[...], axis=0)
    norm2 = jnp.sum(jnp.sum(corr * corr, axis=1, keepdims=True), axis=0, keepdims=True)
    norm = jnp.sqrt(norm2)
    iterate = unflatten16(corr)[:, :16] / norm
    identity = jnp.where(iota((16, 16), 0) == iota((16, 16), 1), 1.0, 0.0).astype(F32)
    inverse = identity
    for sweep in range(NS_ITERS):
        middle = 1.5 * identity - 0.5 * dot32(inverse, iterate)
        iterate = dot32(iterate, middle)
        inverse = dot32(middle, inverse)
        if sweep == 2:
            await_shares(hx, hx_send, hx_recv, ax, 8)
            hy[ay] = jnp.sum(hx[...], axis=0)
            share(hy, hy_send, hy_recv, ay, 16, place_y)
    coeffs = inverse / jnp.sqrt(norm)

    wide = jnp.concatenate([coeffs] * 8, axis=1)
    columns = []
    for o in range(2):
        chosen = iota((16, 128), 1) == 2 * band + o
        column = jnp.sum(jnp.where(chosen, wide, 0.0), axis=1, keepdims=True)
        columns.append(jnp.broadcast_to(column, (16, 128)))
    await_shares(gathered, g_send, g_recv, band, BANDS)
    upper = iota((8, 128), 0) < 4

    def row(o, j):
        return jnp.broadcast_to(columns[o][j : j + 1], (8, 128))

    rotated = jnp.zeros((8, 8, 128), F32)
    for b in range(BANDS):
        block = gathered[b]
        straight = jnp.where(upper, row(0, 2 * b), row(1, 2 * b + 1))
        crossed = jnp.where(upper, row(0, 2 * b + 1), row(1, 2 * b))
        rotated = rotated + straight[None] * block + crossed[None] * roll(block, 4, 1)
    rot_out[0] = rotated[:, 0:4, :]
    rot_out[1] = rotated[:, 4:8, :]

    await_shares(hy, hy_send, hy_recv, ay, 16)
    hmat = unflatten16(jnp.sum(hy[...], axis=0))[:, :16]
    left = lax.dot_general(
        coeffs, hmat, (((0,), (0,)), ((), ())), precision=lax.Precision.HIGHEST, preferred_element_type=F32
    )
    prj_out[...] = dot32(left, coeffs)

    for copy in started:
        copy.wait_send()


def local(orbitals, potential, support, proj, offsets, coupling):
    dma = pltpu.SemaphoreType.DMA
    vmem = pl.BlockSpec(memory_space=pltpu.VMEM)
    smem = pl.BlockSpec(memory_space=pltpu.SMEM)
    block = (8, 8, 128)
    scratch = [
        pltpu.VMEM((ROUNDS,) + block, F32),
        pltpu.VMEM((PBLK,) + block, F32),
        pltpu.VMEM((640, 128), BF16),
        *[pltpu.VMEM((ROUNDS, 4, 8, 128), F32)] * 2,
        *[pltpu.VMEM((ROUNDS, 2, 8, 128), F32)] * 2,
        *[pltpu.VMEM((ROUNDS, 6, 8, 128), F32)] * 2,
        *[pltpu.VMEM((ROUNDS, 4, 8, 128), F32)] * 2,
        *[pltpu.VMEM((ROUNDS, 2, 8, 128), F32)] * 2,
        pltpu.VMEM((ROUNDS, 5, 1, 128), F32),
        pltpu.VMEM(block, F32),
        pltpu.VMEM(block, F32),
        pltpu.VMEM(block, F32),
        pltpu.VMEM((BANDS,) + block, F32),
        *[pltpu.VMEM((n, 2, 128), F32) for n in (8, 8, 16)] * 2,
        *[dma((ROUNDS, 6))] * 2,
        *[dma((ROUNDS, 5))] * 2,
        *[dma((BANDS,))] * 6,
        *[dma((n,)) for n in (8, 8, 8, 8, 16, 16)] * 2,
    ]
    rotated, projected = pl.pallas_call(
        kernel,
        out_shape=(
            jax.ShapeDtypeStruct((2, 8, 4, 128), F32),
            jax.ShapeDtypeStruct((16, 16), F32),
        ),
        in_specs=[vmem, vmem, vmem, vmem, smem, smem],
        out_specs=(vmem, vmem),
        scratch_shapes=scratch,
        compiler_params=pltpu.CompilerParams(
            collective_id=0, has_side_effects=True, vmem_limit_bytes=16 * 1024 * 1024
        ),
    )(
        orbitals.reshape(2, 8, 4, 128),
        potential.reshape(8, 4, 128),
        support.reshape(1, SUPP),
        proj,
        offsets,
        coupling,
    )
    return rotated.reshape(orbitals.shape), projected


def solution(mesh):
    return jax.shard_map(
        local,
        mesh=mesh,
        in_specs=(P("band", "dom", None), P("dom", None), P("dom"), P(None, "dom"), P(), P()),
        out_specs=(P("band", "dom", None), P()),
        check_vma=False,
    )
```

```python
import functools

import jax
import jax.numpy as jnp
from jax import lax
from jax.experimental import pallas as pl
from jax.experimental.pallas import tpu as pltpu
from jax.sharding import PartitionSpec as P

DEG = 4
ROUNDS = DEG + 1
NS_ITERS = 10
NPROJ = 1024
PBLK = 16
SUPP = 512
DOMS = 128
BANDS = 8

STENCIL = [
    -5369.0 / 1800.0,
    12.0 / 7.0,
    -15.0 / 56.0,
    10.0 / 189.0,
    -1.0 / 112.0,
    2.0 / 1925.0,
    -1.0 / 16632.0,
]
HALF = [-0.5 * c for c in STENCIL]
CENTER = 10.0
HALF_WIDTH = 6.0
F32 = jnp.float32
BF16 = jnp.bfloat16
NT = (((1,), (1,)), ((), ()))


def roll(v, shift, axis):
    return pltpu.roll(v, shift % v.shape[axis], axis)


def iota(shape, axis):
    return lax.broadcasted_iota(jnp.int32, shape, axis)


def split3(v):
    high = v.astype(BF16)
    rest = v - high.astype(F32)
    mid = rest.astype(BF16)
    low = (rest - mid.astype(F32)).astype(BF16)
    return high, mid, low


def small_dot(a, b, order=range(16)):
    terms = [
        jnp.broadcast_to(a[:, col : col + 1], (16, 128)) * jnp.broadcast_to(b[r : r + 1, :], (16, 128))
        for r, col in enumerate(order)
    ]
    while len(terms) > 1:
        terms = [x + y for x, y in zip(terms[::2], terms[1::2])]
    return terms[0]


def lane_z(shape):
    return iota(shape, len(shape) - 1) % 32


def lane_y(shape):
    return iota(shape, len(shape) - 1) // 32


def row_y(shape):
    return iota(shape, len(shape) - 2) % 4


def pack_y(v):
    pairs = v.reshape(4, 2, 8, 128)
    even, odd = pairs[:, 0], pairs[:, 1]
    yhi = row_y(even.shape)
    swapped = roll(even, 4, 1)
    first = jnp.where(yhi < 2, swapped, roll(odd, 6, 1))
    last = jnp.where(yhi >= 2, swapped, roll(odd, 2, 1))
    return first, last


def unpack_y(first, last):
    below = jnp.stack([last, roll(last, 2, 1)], axis=1).reshape(8, 8, 128)
    above = jnp.stack([first, roll(first, 6, 1)], axis=1).reshape(8, 8, 128)
    return below, above


def pack_z(v):
    quads = v.reshape(2, 4, 8, 128)
    z = lane_z((2, 8, 128))
    first, last = quads[:, 0], roll(quads[:, 0], 104, 2)
    for i in range(1, 4):
        inside = (z >= 8 * i) & (z < 8 * i + 8)
        first = jnp.where(inside, roll(quads[:, i], 8 * i, 2), first)
        last = jnp.where(inside, roll(quads[:, i], 104 + 8 * i, 2), last)
    return first, last


def unpack_z(first, last):
    above = jnp.stack([roll(first, 32 - 8 * i, 2) for i in range(4)], axis=1)
    below = jnp.stack([roll(last, 120 - 8 * i, 2) for i in range(4)], axis=1)
    return below.reshape(8, 8, 128), above.reshape(8, 8, 128)


def sum_x(v, below, above):
    ext = jnp.concatenate([below, v, above], axis=0)
    total = HALF[1] * (ext[7:15] + ext[5:13])
    for k in range(2, 7):
        total = total + HALF[k] * (ext[6 + k : 14 + k] + ext[6 - k : 14 - k])
    return total


def sum_y(v, below, above):
    yhi = row_y(v.shape)
    up1 = roll(jnp.where(yhi < 1, above, v), 7, 1)
    up2 = roll(jnp.where(yhi < 2, above, v), 6, 1)
    dn1 = roll(jnp.where(yhi >= 3, below, v), 1, 1)
    dn2 = roll(jnp.where(yhi >= 2, below, v), 2, 1)
    p = lane_y((1, 8, 128))
    h = HALF

    def pick(edge, upper, lower):
        return jnp.where(p >= edge, jnp.float32(upper), jnp.float32(lower))

    one = (
        pick(1, h[1], h[3]) * v
        + pick(1, h[5], h[1]) * up1
        + pick(1, 0.0, h[5]) * up2
        + pick(1, h[3], 0.0) * dn1
    )
    two = (
        h[2] * v
        + pick(2, h[6], h[2]) * up1
        + pick(2, 0.0, h[6]) * up2
        + pick(2, h[2], h[6]) * dn1
        + pick(2, h[6], 0.0) * dn2
    )
    three = (
        pick(3, h[3], h[1]) * v
        + pick(3, 0.0, h[3]) * up1
        + pick(3, h[1], h[5]) * dn1
        + pick(3, h[5], 0.0) * dn2
    )
    return h[4] * (up1 + dn1) + roll(one, 96, 2) + roll(two, 64, 2) + roll(three, 32, 2)


def sum_z(v, below, above):
    z = lane_z(v.shape)
    total = None
    for k in range(1, 7):
        up = roll(jnp.where(z < k, above, v), 128 - k, 2)
        down = roll(jnp.where(z >= 32 - k, below, v), k, 2)
        term = HALF[k] * (up + down)
        total = term if total is None else total + term
    return total


def spread_projectors(support, proj):
    high_bits = support // 128
    low_bits = support % 128
    rows = (iota((32, SUPP), 0) == high_bits).astype(F32)
    lanes = (iota((128, SUPP), 0) == low_bits).astype(F32).astype(BF16)
    dense = None
    for part in split3(proj):
        left = (part.astype(F32)[:, None, :] * rows[None]).reshape(PBLK * 32, SUPP)
        term = lax.dot_general(left.astype(BF16), lanes, NT, preferred_element_type=F32)
        dense = term if dense is None else dense + term
    dense = dense.reshape(PBLK * 4, 8, 128)
    turned = roll(dense, 4, 1)
    upper = iota(dense.shape, 1) < 4
    even = jnp.where(upper, dense, turned)
    odd = jnp.where(upper, turned, dense)
    return jnp.stack([even, odd], axis=1).reshape(PBLK, 8, 8, 128)


def lane_sums(rows):
    parts = jnp.concatenate(split3(rows), axis=1)
    return lax.dot_general(jnp.ones((8, 384), BF16), parts, NT, preferred_element_type=F32)[0:1]


def square(rows):
    lane, line = iota((16, 128), 1), iota((16, 128), 0)
    spread = jnp.concatenate([jnp.broadcast_to(rows[z : z + 1], (2, 128)) for z in range(BANDS)], axis=0)
    spread = jnp.where((lane // 8) % 2 == line % 2, spread, 0.0)
    source, target = iota((128, 128), 0), iota((128, 128), 1)
    fold = jnp.where(target % 16 == 2 * (source // 16) + (source // 4) % 2, 1.0, 0.0).astype(BF16)
    parts = jnp.concatenate(split3(spread), axis=0)
    three = jnp.dot(parts, fold, preferred_element_type=F32)
    half = three[0:16] + three[16:32] + three[32:48]
    turned = jnp.concatenate([jnp.transpose(half)[0:16, 0:16]] * 8, axis=1)
    return jnp.where((lane % 16) // 2 <= line // 2, half, turned)


def kernel(
    orb_hbm, pot_hbm, sup_hbm, proj_hbm, off_hbm, coup_hbm, rot_out, prj_out,
    orb, pot, sup, proj, off, coup, load_sem,
    ys, pdense, match, yfirst, ylast, zfirst, zlast,
    xbelow, xabove, ybelow, yabove, zbelow, zabove, inner,
    earlier, later, cx, cy, cz, hx, hy, hz,
    halo_send, halo_recv, inner_send, inner_recv, g_send, g_recv,
    cx_send, cx_recv, cy_send, cy_recv, cz_send, cz_recv,
    hx_send, hx_recv, hy_send, hy_recv, hz_send, hz_recv, later_in,
):
    me = lax.axis_index("dom")
    band = lax.axis_index("band")
    ax, ay = me // 16, me % 16
    by, cz_pos = (me // 4) % 4, me % 4

    def dom_x(i):
        return ((ax + i) % 8) * 16 + ay

    def dom_y(i):
        return ax * 16 + (ay + i) % 16

    x_up, x_down = dom_x(1), dom_x(7)
    y_up = ax * 16 + ((by + 1) % 4) * 4 + cz_pos
    y_down = ax * 16 + ((by + 3) % 4) * 4 + cz_pos
    z_up = me - cz_pos + (cz_pos + 1) % 4
    z_down = me - cz_pos + (cz_pos + 3) % 4
    chain = [((me + step) % DOMS, 2 - step) for step in (-2 + DOMS, -1 + DOMS, 1, 2)]
    chain = [(dom, slot + DOMS if slot < 0 else slot) for dom, slot in chain]

    barrier = pltpu.get_barrier_semaphore()
    near = [(y_up, band), (y_down, band)] + [(dom, band) for dom, _ in chain]
    near += [(x_up, band), (x_down, band), (z_up, band), (z_down, band)]
    for device in near:
        pl.semaphore_signal(barrier, inc=1, device_id=device, device_id_type=pl.DeviceIdType.MESH)
    for b in range(1, BANDS):
        @pl.when(b > band)
        def _(b=b):
            pl.semaphore_signal(barrier, inc=1, device_id=(me, b), device_id_type=pl.DeviceIdType.MESH)

    loads = []
    for i, (src, dst) in enumerate(
        [(orb_hbm, orb), (proj_hbm, proj), (sup_hbm, sup), (off_hbm, off), (pot_hbm, pot), (coup_hbm, coup)]
    ):
        loads.append(pltpu.make_async_copy(src, dst, load_sem.at[i]))
        loads[-1].start()

    started = []

    def send(src, dst, ssem, rsem, dom, to_band):
        copy = pltpu.make_async_remote_copy(
            src_ref=src, dst_ref=dst, send_sem=ssem, recv_sem=rsem,
            device_id=(dom, to_band), device_id_type=pl.DeviceIdType.MESH,
        )
        copy.start()
        started.append(copy)

    def await_copy(src, dst, ssem, rsem):
        pltpu.make_async_remote_copy(
            src_ref=src, dst_ref=dst, send_sem=ssem, recv_sem=rsem,
            device_id=(me, band), device_id_type=pl.DeviceIdType.MESH,
        ).wait_recv()

    def share(buf, ssem, rsem, pos, count, place):
        for i in range(1, count):
            dom, to_band = place(i)
            send(buf.at[pos], buf.at[pos], ssem.at[i], rsem.at[pos], dom, to_band)

    def await_shares(buf, ssem, rsem, pos, count):
        for i in range(1, count):
            source = (pos + count - i) % count
            await_copy(buf.at[source], buf.at[source], ssem.at[i], rsem.at[source])

    def band_copy(b, buf):
        return pltpu.make_async_remote_copy(
            src_ref=ys.at[DEG], dst_ref=buf.at[band], send_sem=g_send.at[b], recv_sem=g_recv.at[band],
            device_id=(me, b), device_id_type=pl.DeviceIdType.MESH,
        )

    def place_z(i):
        return me, (band + i) % BANDS

    def place_x(i):
        return dom_x(i), band

    def place_y(i):
        return dom_y(i), band

    def pack(k, v):
        yfirst[k], ylast[k] = pack_y(v)
        zfirst[k], zlast[k] = pack_z(v)

    def send_far(k):
        block = ys.at[k]
        hs, hr = halo_send.at[k], halo_recv.at[k]
        send(yfirst.at[k], yabove.at[k], hs.at[0], hr.at[0], y_down, band)
        send(ylast.at[k], ybelow.at[k], hs.at[1], hr.at[1], y_up, band)
        send(block.at[pl.ds(0, 6)], xabove.at[k], hs.at[2], hr.at[2], x_down, band)
        send(block.at[pl.ds(2, 6)], xbelow.at[k], hs.at[3], hr.at[3], x_up, band)

    def send_near(k):
        hs, hr = halo_send.at[k], halo_recv.at[k]
        send(zfirst.at[k], zabove.at[k], hs.at[4], hr.at[4], z_down, band)
        send(zlast.at[k], zbelow.at[k], hs.at[5], hr.at[5], z_up, band)

    def project(k, v):
        inner[k, 2] = lane_sums(
            jnp.concatenate([jnp.sum(pdense[j] * v, axis=0) for j in range(PBLK)], axis=0)
        )

    def send_inner(k):
        for i, (dom, slot) in enumerate(chain):
            send(inner.at[k, 2], inner.at[k, slot], inner_send.at[k, i], inner_recv.at[k, slot], dom, band)

    def exchange(k, v):
        pack(k, v)
        send_far(k)
        project(k, v)
        send_inner(k)
        send_near(k)

    def apply_h(k, v, own, couple):
        hs, hr = halo_send.at[k], halo_recv.at[k]
        await_copy(zabove.at[k], zabove.at[k], hs.at[4], hr.at[4])
        await_copy(zbelow.at[k], zbelow.at[k], hs.at[5], hr.at[5])
        field = own * v + sum_z(v, *unpack_z(zabove[k], zbelow[k]))
        await_copy(xabove.at[k], xabove.at[k], hs.at[2], hr.at[2])
        await_copy(xbelow.at[k], xbelow.at[k], hs.at[3], hr.at[3])
        field = field + sum_x(v, xbelow[k], xabove[k])
        await_copy(yabove.at[k], yabove.at[k], hs.at[0], hr.at[0])
        await_copy(ybelow.at[k], ybelow.at[k], hs.at[1], hr.at[1])
        field = field + sum_y(v, *unpack_y(yabove[k], ybelow[k]))
        for i, (_, slot) in enumerate(chain):
            slot = 4 - slot
            await_copy(inner.at[k, slot], inner.at[k, slot], inner_send.at[k, i], inner_recv.at[k, slot])
        rows = jnp.concatenate([inner[k, slot] for slot in range(5)], axis=1)
        mine = (iota((8, 640), 1) // 4) % 2 == iota((8, 640), 0) // 4
        rows = jnp.where(mine, jnp.broadcast_to(rows, (8, 640)), 0.0)
        parts = [part.astype(F32) for part in split3(rows)]
        stacked = jnp.concatenate(parts + [jnp.zeros((8, 640), F32)], axis=0).astype(BF16)
        totals = jnp.dot(stacked, match[...], preferred_element_type=F32)
        coefs = (totals[0:8] + totals[8:16] + totals[16:24]) * couple
        for j in range(PBLK):
            field = field + jnp.broadcast_to(coefs[:, j : j + 1], (8, 128))[None] * pdense[j]
        return field

    for load in loads:
        load.wait()
    ys[0, :, 0:4, :] = orb[0]
    ys[0, :, 4:8, :] = orb[1]
    current = ys[0]
    pack(0, current)
    pdense[...] = spread_projectors(sup[...], proj[...])
    project(0, current)
    for b in range(BANDS):
        @pl.when(b > band)
        def _(b=b):
            earlier[b] = jnp.zeros((8, 8, 128), F32)

        @pl.when(b <= band)
        def _(b=b):
            later[b] = jnp.zeros((8, 8, 128), F32)

    pl.semaphore_wait(barrier, len(near) + band)
    send_far(0)
    send_inner(0)
    send_near(0)
    for b in range(BANDS - 1):
        @pl.when(b < band)
        def _(b=b):
            pl.semaphore_signal(later_in, inc=1, device_id=(me, b), device_id_type=pl.DeviceIdType.MESH)

    pots = jnp.concatenate([pot[...], pot[...]], axis=1)
    own = pots + jnp.float32(3.0 * HALF[0])
    first_id = off[me]
    couple = jnp.zeros((1, 128), F32)
    lane = iota((1, 128), 1)
    for j in range(PBLK):
        couple = jnp.where(lane == j, coup[(first_id + j) % NPROJ], couple)
    wanted = (first_id + iota((128, 128), 1)) % NPROJ
    for slot in range(5):
        theirs = off[(me + slot - 2 + DOMS) % DOMS]
        have = (theirs + iota((128, 128), 0) // 8) % NPROJ
        match[slot * 128 : slot * 128 + 128, :] = jnp.where(have == wanted, 1.0, 0.0).astype(BF16)

    previous = current
    current = (apply_h(0, current, own, couple) - CENTER * current) * (1.0 / HALF_WIDTH)
    for k in range(1, DEG):
        ys[k] = current
        exchange(k, current)
        following = (apply_h(k, current, own, couple) - CENTER * current) * (2.0 / HALF_WIDTH) - previous
        previous, current = current, following
    ys[DEG] = current

    @pl.when(band < BANDS - 1)
    def _():
        pl.semaphore_wait(later_in, BANDS - 1 - band)

    earlier[band] = current
    exchange(DEG, current)
    for b in reversed(range(BANDS)):
        @pl.when(b > band)
        def _(b=b):
            band_copy(b, earlier).start()

        @pl.when(b < band)
        def _(b=b):
            band_copy(b, later).start()

    def columns_of(v):
        upper = iota(v.shape, 1) < 4
        other = roll(v, 4, 1)
        both = [jnp.where(upper, v, other), jnp.where(upper, other, v)]
        return lane_sums(
            jnp.concatenate([jnp.sum(earlier[b] * both[o], axis=0) for b in range(BANDS) for o in range(2)], axis=0)
        )

    for b in range(BANDS - 1):
        @pl.when(b < band)
        def _(b=b):
            await_copy(earlier.at[b], earlier.at[b], g_send.at[b], g_recv.at[b])

    cx[ax] = columns_of(current)
    share(cx, cx_send, cx_recv, ax, 8, place_x)
    hfield = apply_h(DEG, current, own, couple)
    hx[ax] = columns_of(hfield)
    share(hx, hx_send, hx_recv, ax, 8, place_x)
    await_shares(cx, cx_send, cx_recv, ax, 8)
    cy[ay] = jnp.sum(cx[...], axis=0)
    share(cy, cy_send, cy_recv, ay, 16, place_y)
    await_shares(hx, hx_send, hx_recv, ax, 8)
    hy[ay] = jnp.sum(hx[...], axis=0)
    share(hy, hy_send, hy_recv, ay, 16, place_y)
    await_shares(cy, cy_send, cy_recv, ay, 16)
    cz[band] = jnp.sum(cy[...], axis=0)
    share(cz, cz_send, cz_recv, band, BANDS, place_z)
    await_shares(hy, hy_send, hy_recv, ay, 16)
    hz[band] = jnp.sum(hy[...], axis=0)
    share(hz, hz_send, hz_recv, band, BANDS, place_z)
    await_shares(cz, cz_send, cz_recv, band, BANDS)
    corr = square(jnp.concatenate([cz[b] for b in range(BANDS)], axis=0))

    norm2 = jnp.sum(jnp.sum(corr * corr, axis=1, keepdims=True), axis=0, keepdims=True) * 0.125
    norm = jnp.sqrt(norm2)
    identity = jnp.where(iota((16, 128), 0) == iota((16, 128), 1) % 16, 1.0, 0.0).astype(F32)

    def sweep(_, pair):
        iterate, inverse = pair
        middle = 1.5 * identity - 0.5 * small_dot(inverse, iterate)
        return small_dot(iterate, middle), small_dot(middle, inverse)

    _, inverse = lax.fori_loop(0, NS_ITERS, sweep, (corr / norm, identity))
    coeffs = inverse / jnp.sqrt(norm)

    columns = []
    for o in range(2):
        chosen = iota((16, 128), 1) == 2 * band + o
        column = jnp.sum(jnp.where(chosen, coeffs, 0.0), axis=1, keepdims=True)
        columns.append(jnp.broadcast_to(column, (16, 128)))
    upper = iota((8, 128), 0) < 4

    def row(o, j):
        return jnp.broadcast_to(columns[o][j : j + 1], (8, 128))

    for b in range(1, BANDS):
        @pl.when(b > band)
        def _(b=b):
            await_copy(later.at[b], later.at[b], g_send.at[b], g_recv.at[b])

    rotated = jnp.zeros((8, 8, 128), F32)
    for b in range(BANDS):
        block = earlier[b] + later[b]
        straight = jnp.where(upper, row(0, 2 * b), row(1, 2 * b + 1))
        crossed = jnp.where(upper, row(0, 2 * b + 1), row(1, 2 * b))
        rotated = rotated + straight[None] * block + crossed[None] * roll(block, 4, 1)
    rot_out[0] = rotated[:, 0:4, :]
    rot_out[1] = rotated[:, 4:8, :]

    await_shares(hz, hz_send, hz_recv, band, BANDS)
    hmat = square(jnp.concatenate([hz[b] for b in range(BANDS)], axis=0))
    prj_out[...] = small_dot(small_dot(coeffs, hmat), coeffs)[:, 0:16]

    for b in range(BANDS):
        @pl.when(b != band)
        def _(b=b):
            band_copy(b, earlier).wait_send()

    for copy in started:
        copy.wait_send()


def local(orbitals, potential, support, proj, offsets, coupling):
    dma = pltpu.SemaphoreType.DMA
    vmem = pl.BlockSpec(memory_space=pltpu.VMEM)
    anywhere = pl.BlockSpec(memory_space=pl.ANY)
    block = (8, 8, 128)
    scratch = [
        pltpu.VMEM((2, 8, 4, 128), F32),
        pltpu.VMEM((8, 4, 128), F32),
        pltpu.VMEM((1, SUPP), jnp.int32),
        pltpu.VMEM((PBLK, SUPP), F32),
        pltpu.SMEM((DOMS,), jnp.int32),
        pltpu.SMEM((NPROJ,), F32),
        dma((6,)),
        pltpu.VMEM((ROUNDS,) + block, F32),
        pltpu.VMEM((PBLK,) + block, F32),
        pltpu.VMEM((640, 128), BF16),
        *[pltpu.VMEM((ROUNDS, 4, 8, 128), F32)] * 2,
        *[pltpu.VMEM((ROUNDS, 2, 8, 128), F32)] * 2,
        *[pltpu.VMEM((ROUNDS, 6, 8, 128), F32)] * 2,
        *[pltpu.VMEM((ROUNDS, 4, 8, 128), F32)] * 2,
        *[pltpu.VMEM((ROUNDS, 2, 8, 128), F32)] * 2,
        pltpu.VMEM((ROUNDS, 5, 1, 128), F32),
        *[pltpu.VMEM((BANDS,) + block, F32)] * 2,
        *[pltpu.VMEM((n, 1, 128), F32) for n in (8, 16, 8)] * 2,
        *[dma((ROUNDS, 6))] * 2,
        *[dma((ROUNDS, 5))] * 2,
        *[dma((BANDS,))] * 2,
        *[dma((n,)) for n in (8, 8, 16, 16, 8, 8)] * 2,
        pltpu.SemaphoreType.REGULAR,
    ]
    rotated, projected = pl.pallas_call(
        kernel,
        out_shape=(
            jax.ShapeDtypeStruct((2, 8, 4, 128), F32),
            jax.ShapeDtypeStruct((16, 16), F32),
        ),
        in_specs=[anywhere] * 6,
        out_specs=(vmem, vmem),
        scratch_shapes=scratch,
        compiler_params=pltpu.CompilerParams(
            collective_id=0, has_side_effects=True, vmem_limit_bytes=60 * 1024 * 1024
        ),
    )(
        orbitals.reshape(2, 8, 4, 128),
        potential.reshape(8, 4, 128),
        support.reshape(1, SUPP),
        proj,
        offsets,
        coupling,
    )
    return rotated.reshape(orbitals.shape), projected


def solution(mesh):
    return jax.shard_map(
        local,
        mesh=mesh,
        in_specs=(P("band", "dom", None), P("dom", None), P("dom"), P(None, "dom"), P(), P()),
        out_specs=(P("band", "dom", None), P()),
        check_vma=False,
    )
```

```python
import functools

import jax
import jax.numpy as jnp
from jax import lax
from jax.experimental import pallas as pl
from jax.experimental.pallas import tpu as pltpu
from jax.sharding import PartitionSpec as P

DEG = 4
ROUNDS = DEG + 1
NS_ITERS = 10
NPROJ = 1024
PBLK = 16
SUPP = 512
DOMS = 128
BANDS = 8

STENCIL = [
    -5369.0 / 1800.0,
    12.0 / 7.0,
    -15.0 / 56.0,
    10.0 / 189.0,
    -1.0 / 112.0,
    2.0 / 1925.0,
    -1.0 / 16632.0,
]
HALF = [-0.5 * c for c in STENCIL]
CENTER = 10.0
HALF_WIDTH = 6.0
F32 = jnp.float32
BF16 = jnp.bfloat16
NT = (((1,), (1,)), ((), ()))


def roll(v, shift, axis):
    return pltpu.roll(v, shift % v.shape[axis], axis)


def iota(shape, axis):
    return lax.broadcasted_iota(jnp.int32, shape, axis)


def split3(v):
    high = v.astype(BF16)
    rest = v - high.astype(F32)
    mid = rest.astype(BF16)
    low = (rest - mid.astype(F32)).astype(BF16)
    return high, mid, low


def small_dot(a, b, order=range(16)):
    terms = [
        jnp.broadcast_to(a[:, col : col + 1], (16, 128)) * jnp.broadcast_to(b[r : r + 1, :], (16, 128))
        for r, col in enumerate(order)
    ]
    while len(terms) > 1:
        terms = [x + y for x, y in zip(terms[::2], terms[1::2])]
    return terms[0]


def lane_z(shape):
    return iota(shape, len(shape) - 1) % 32


def lane_y(shape):
    return iota(shape, len(shape) - 1) // 32


def row_y(shape):
    return iota(shape, len(shape) - 2) % 4


def pack_y(v):
    pairs = v.reshape(4, 2, 8, 128)
    even, odd = pairs[:, 0], pairs[:, 1]
    yhi = row_y(even.shape)
    swapped = roll(even, 4, 1)
    first = jnp.where(yhi < 2, swapped, roll(odd, 6, 1))
    last = jnp.where(yhi >= 2, swapped, roll(odd, 2, 1))
    return first, last


def unpack_y(first, last):
    below = jnp.stack([last, roll(last, 2, 1)], axis=1).reshape(8, 8, 128)
    above = jnp.stack([first, roll(first, 6, 1)], axis=1).reshape(8, 8, 128)
    return below, above


def pack_z(v):
    quads = v.reshape(2, 4, 8, 128)
    z = lane_z((2, 8, 128))
    first, last = quads[:, 0], roll(quads[:, 0], 104, 2)
    for i in range(1, 4):
        inside = (z >= 8 * i) & (z < 8 * i + 8)
        first = jnp.where(inside, roll(quads[:, i], 8 * i, 2), first)
        last = jnp.where(inside, roll(quads[:, i], 104 + 8 * i, 2), last)
    return first, last


def unpack_z(first, last):
    above = jnp.stack([roll(first, 32 - 8 * i, 2) for i in range(4)], axis=1)
    below = jnp.stack([roll(last, 120 - 8 * i, 2) for i in range(4)], axis=1)
    return below.reshape(8, 8, 128), above.reshape(8, 8, 128)


def sum_x(v, below, above):
    ext = jnp.concatenate([below, v, above], axis=0)
    total = HALF[1] * (ext[7:15] + ext[5:13])
    for k in range(2, 7):
        total = total + HALF[k] * (ext[6 + k : 14 + k] + ext[6 - k : 14 - k])
    return total


def sum_y(v, below, above):
    yhi = row_y(v.shape)
    up1 = roll(jnp.where(yhi < 1, above, v), 7, 1)
    up2 = roll(jnp.where(yhi < 2, above, v), 6, 1)
    dn1 = roll(jnp.where(yhi >= 3, below, v), 1, 1)
    dn2 = roll(jnp.where(yhi >= 2, below, v), 2, 1)
    p = lane_y((1, 8, 128))
    h = HALF

    def pick(edge, upper, lower):
        return jnp.where(p >= edge, jnp.float32(upper), jnp.float32(lower))

    one = (
        pick(1, h[1], h[3]) * v
        + pick(1, h[5], h[1]) * up1
        + pick(1, 0.0, h[5]) * up2
        + pick(1, h[3], 0.0) * dn1
    )
    two = (
        h[2] * v
        + pick(2, h[6], h[2]) * up1
        + pick(2, 0.0, h[6]) * up2
        + pick(2, h[2], h[6]) * dn1
        + pick(2, h[6], 0.0) * dn2
    )
    three = (
        pick(3, h[3], h[1]) * v
        + pick(3, 0.0, h[3]) * up1
        + pick(3, h[1], h[5]) * dn1
        + pick(3, h[5], 0.0) * dn2
    )
    return h[4] * (up1 + dn1) + roll(one, 96, 2) + roll(two, 64, 2) + roll(three, 32, 2)


def sum_z(v, below, above):
    z = lane_z(v.shape)
    total = None
    for k in range(1, 7):
        up = roll(jnp.where(z < k, above, v), 128 - k, 2)
        down = roll(jnp.where(z >= 32 - k, below, v), k, 2)
        term = HALF[k] * (up + down)
        total = term if total is None else total + term
    return total


def spread_projectors(support, proj):
    high_bits = support // 128
    low_bits = support % 128
    rows = (iota((32, SUPP), 0) == high_bits).astype(F32)
    lanes = (iota((128, SUPP), 0) == low_bits).astype(F32).astype(BF16)
    dense = None
    for part in split3(proj):
        left = (part.astype(F32)[:, None, :] * rows[None]).reshape(PBLK * 32, SUPP)
        term = lax.dot_general(left.astype(BF16), lanes, NT, preferred_element_type=F32)
        dense = term if dense is None else dense + term
    dense = dense.reshape(PBLK * 4, 8, 128)
    turned = roll(dense, 4, 1)
    upper = iota(dense.shape, 1) < 4
    even = jnp.where(upper, dense, turned)
    odd = jnp.where(upper, turned, dense)
    return jnp.stack([even, odd], axis=1).reshape(PBLK, 8, 8, 128)


def lane_sums(rows):
    parts = jnp.concatenate(split3(rows), axis=1)
    return lax.dot_general(jnp.ones((8, 384), BF16), parts, NT, preferred_element_type=F32)[0:1]


def square(rows):
    lane, line = iota((16, 128), 1), iota((16, 128), 0)
    spread = jnp.concatenate([jnp.broadcast_to(rows[z : z + 1], (2, 128)) for z in range(BANDS)], axis=0)
    spread = jnp.where((lane // 8) % 2 == line % 2, spread, 0.0)
    source, target = iota((128, 128), 0), iota((128, 128), 1)
    fold = jnp.where(target % 16 == 2 * (source // 16) + (source // 4) % 2, 1.0, 0.0).astype(BF16)
    parts = jnp.concatenate(split3(spread), axis=0)
    three = jnp.dot(parts, fold, preferred_element_type=F32)
    half = three[0:16] + three[16:32] + three[32:48]
    turned = jnp.concatenate([jnp.transpose(half)[0:16, 0:16]] * 8, axis=1)
    return jnp.where((lane % 16) // 2 <= line // 2, half, turned)


def kernel(
    orb_hbm, pot_hbm, sup_hbm, proj_hbm, off_hbm, coup_hbm, rot_out, prj_out,
    orb, pot, sup, proj, off, coup, load_sem,
    ys, pdense, match, yfirst, ylast, zfirst, zlast,
    xbelow, xabove, ybelow, yabove, zbelow, zabove, inner,
    earlier, later, cx, cy, cz, hx, hy, hz,
    halo_send, halo_recv, inner_send, inner_recv, g_send, g_recv,
    cx_send, cx_recv, cy_send, cy_recv, cz_send, cz_recv,
    hx_send, hx_recv, hy_send, hy_recv, hz_send, hz_recv, later_in,
):
    me = lax.axis_index("dom")
    band = lax.axis_index("band")
    ax, ay = me // 16, me % 16
    by, cz_pos = (me // 4) % 4, me % 4

    def dom_x(i):
        return ((ax + i) % 8) * 16 + ay

    def dom_y(i):
        return ax * 16 + (ay + i) % 16

    x_up, x_down = dom_x(1), dom_x(7)
    y_up = ax * 16 + ((by + 1) % 4) * 4 + cz_pos
    y_down = ax * 16 + ((by + 3) % 4) * 4 + cz_pos
    z_up = me - cz_pos + (cz_pos + 1) % 4
    z_down = me - cz_pos + (cz_pos + 3) % 4
    chain = [((me + step) % DOMS, 2 - step) for step in (-2 + DOMS, -1 + DOMS, 1, 2)]
    chain = [(dom, slot + DOMS if slot < 0 else slot) for dom, slot in chain]

    barrier = pltpu.get_barrier_semaphore()
    near = [(y_up, band), (y_down, band)] + [(dom, band) for dom, _ in chain]
    near += [(x_up, band), (x_down, band), (z_up, band), (z_down, band)]
    for device in near:
        pl.semaphore_signal(barrier, inc=1, device_id=device, device_id_type=pl.DeviceIdType.MESH)
    for b in range(1, BANDS):
        @pl.when(b > band)
        def _(b=b):
            pl.semaphore_signal(barrier, inc=1, device_id=(me, b), device_id_type=pl.DeviceIdType.MESH)

    loads = []
    for i, (src, dst) in enumerate(
        [(orb_hbm, orb), (proj_hbm, proj), (sup_hbm, sup), (off_hbm, off), (pot_hbm, pot), (coup_hbm, coup)]
    ):
        loads.append(pltpu.make_async_copy(src, dst, load_sem.at[i]))
        loads[-1].start()

    started = []

    def send(src, dst, ssem, rsem, dom, to_band):
        copy = pltpu.make_async_remote_copy(
            src_ref=src, dst_ref=dst, send_sem=ssem, recv_sem=rsem,
            device_id=(dom, to_band), device_id_type=pl.DeviceIdType.MESH,
        )
        copy.start()
        started.append(copy)

    def await_copy(src, dst, ssem, rsem):
        pltpu.make_async_remote_copy(
            src_ref=src, dst_ref=dst, send_sem=ssem, recv_sem=rsem,
            device_id=(me, band), device_id_type=pl.DeviceIdType.MESH,
        ).wait_recv()

    def share(buf, ssem, rsem, pos, count, place):
        for i in sorted(range(1, count), key=lambda i: abs(i - count // 2)):
            dom, to_band = place(i)
            send(buf.at[pos], buf.at[pos], ssem.at[i], rsem.at[pos], dom, to_band)

    def await_shares(buf, ssem, rsem, pos, count):
        for i in range(1, count):
            source = (pos + count - i) % count
            await_copy(buf.at[source], buf.at[source], ssem.at[i], rsem.at[source])

    def band_copy(b, buf):
        return pltpu.make_async_remote_copy(
            src_ref=ys.at[DEG], dst_ref=buf.at[band], send_sem=g_send.at[b], recv_sem=g_recv.at[band],
            device_id=(me, b), device_id_type=pl.DeviceIdType.MESH,
        )

    def place_z(i):
        return me, (band + i) % BANDS

    def place_x(i):
        return dom_x(i), band

    def place_y(i):
        return dom_y(i), band

    def pack(k, v):
        yfirst[k], ylast[k] = pack_y(v)
        zfirst[k], zlast[k] = pack_z(v)

    def send_far(k):
        block = ys.at[k]
        hs, hr = halo_send.at[k], halo_recv.at[k]
        send(yfirst.at[k], yabove.at[k], hs.at[0], hr.at[0], y_down, band)
        send(ylast.at[k], ybelow.at[k], hs.at[1], hr.at[1], y_up, band)
        send(block.at[pl.ds(0, 6)], xabove.at[k], hs.at[2], hr.at[2], x_down, band)
        send(block.at[pl.ds(2, 6)], xbelow.at[k], hs.at[3], hr.at[3], x_up, band)

    def send_near(k):
        hs, hr = halo_send.at[k], halo_recv.at[k]
        send(zfirst.at[k], zabove.at[k], hs.at[4], hr.at[4], z_down, band)
        send(zlast.at[k], zbelow.at[k], hs.at[5], hr.at[5], z_up, band)

    def project(k, v):
        inner[k, 2] = lane_sums(
            jnp.concatenate([jnp.sum(pdense[j] * v, axis=0) for j in range(PBLK)], axis=0)
        )

    def send_inner(k):
        for i, (dom, slot) in enumerate(chain):
            send(inner.at[k, 2], inner.at[k, slot], inner_send.at[k, i], inner_recv.at[k, slot], dom, band)

    def exchange(k, v):
        pack(k, v)
        send_far(k)
        project(k, v)
        send_inner(k)
        send_near(k)

    def apply_h(k, v, own, couple):
        hs, hr = halo_send.at[k], halo_recv.at[k]
        await_copy(zabove.at[k], zabove.at[k], hs.at[4], hr.at[4])
        await_copy(zbelow.at[k], zbelow.at[k], hs.at[5], hr.at[5])
        field = own * v + sum_z(v, *unpack_z(zabove[k], zbelow[k]))
        await_copy(xabove.at[k], xabove.at[k], hs.at[2], hr.at[2])
        await_copy(xbelow.at[k], xbelow.at[k], hs.at[3], hr.at[3])
        field = field + sum_x(v, xbelow[k], xabove[k])
        for i, (_, slot) in enumerate(chain):
            slot = 4 - slot
            await_copy(inner.at[k, slot], inner.at[k, slot], inner_send.at[k, i], inner_recv.at[k, slot])
        rows = jnp.concatenate([inner[k, slot] for slot in range(5)], axis=1)
        mine = (iota((8, 640), 1) // 4) % 2 == iota((8, 640), 0) // 4
        rows = jnp.where(mine, jnp.broadcast_to(rows, (8, 640)), 0.0)
        parts = [part.astype(F32) for part in split3(rows)]
        stacked = jnp.concatenate(parts + [jnp.zeros((8, 640), F32)], axis=0).astype(BF16)
        totals = jnp.dot(stacked, match[...], preferred_element_type=F32)
        coefs = (totals[0:8] + totals[8:16] + totals[16:24]) * couple
        for j in range(PBLK):
            field = field + jnp.broadcast_to(coefs[:, j : j + 1], (8, 128))[None] * pdense[j]
        await_copy(yabove.at[k], yabove.at[k], hs.at[0], hr.at[0])
        await_copy(ybelow.at[k], ybelow.at[k], hs.at[1], hr.at[1])
        field = field + sum_y(v, *unpack_y(yabove[k], ybelow[k]))
        return field

    for load in loads:
        load.wait()
    ys[0, :, 0:4, :] = orb[0]
    ys[0, :, 4:8, :] = orb[1]
    current = ys[0]
    pack(0, current)
    pdense[...] = spread_projectors(sup[...], proj[...])
    project(0, current)
    for b in range(BANDS):
        @pl.when(b > band)
        def _(b=b):
            earlier[b] = jnp.zeros((8, 8, 128), F32)

        @pl.when(b <= band)
        def _(b=b):
            later[b] = jnp.zeros((8, 8, 128), F32)

    pl.semaphore_wait(barrier, len(near) + band)
    send_far(0)
    send_inner(0)
    send_near(0)
    for b in range(BANDS - 1):
        @pl.when(b < band)
        def _(b=b):
            pl.semaphore_signal(later_in, inc=1, device_id=(me, b), device_id_type=pl.DeviceIdType.MESH)

    pots = jnp.concatenate([pot[...], pot[...]], axis=1)
    own = pots + jnp.float32(3.0 * HALF[0])
    first_id = off[me]
    couple = jnp.zeros((1, 128), F32)
    lane = iota((1, 128), 1)
    for j in range(PBLK):
        couple = jnp.where(lane == j, coup[(first_id + j) % NPROJ], couple)
    wanted = (first_id + iota((128, 128), 1)) % NPROJ
    for slot in range(5):
        theirs = off[(me + slot - 2 + DOMS) % DOMS]
        have = (theirs + iota((128, 128), 0) // 8) % NPROJ
        match[slot * 128 : slot * 128 + 128, :] = jnp.where(have == wanted, 1.0, 0.0).astype(BF16)

    previous = current
    current = (apply_h(0, current, own, couple) - CENTER * current) * (1.0 / HALF_WIDTH)
    for k in range(1, DEG):
        ys[k] = current
        exchange(k, current)
        following = (apply_h(k, current, own, couple) - CENTER * current) * (2.0 / HALF_WIDTH) - previous
        previous, current = current, following
    ys[DEG] = current

    @pl.when(band < BANDS - 1)
    def _():
        pl.semaphore_wait(later_in, BANDS - 1 - band)

    earlier[band] = current
    exchange(DEG, current)
    for b in reversed(range(BANDS)):
        @pl.when(b > band)
        def _(b=b):
            band_copy(b, earlier).start()

        @pl.when(b < band)
        def _(b=b):
            band_copy(b, later).start()

    def columns_of(v):
        upper = iota(v.shape, 1) < 4
        other = roll(v, 4, 1)
        both = [jnp.where(upper, v, other), jnp.where(upper, other, v)]
        return lane_sums(
            jnp.concatenate([jnp.sum(earlier[b] * both[o], axis=0) for b in range(BANDS) for o in range(2)], axis=0)
        )

    for b in range(BANDS - 1):
        @pl.when(b < band)
        def _(b=b):
            await_copy(earlier.at[b], earlier.at[b], g_send.at[b], g_recv.at[b])

    cx[ax] = columns_of(current)
    share(cx, cx_send, cx_recv, ax, 8, place_x)
    hfield = apply_h(DEG, current, own, couple)
    hx[ax] = columns_of(hfield)
    share(hx, hx_send, hx_recv, ax, 8, place_x)
    await_shares(cx, cx_send, cx_recv, ax, 8)
    cy[ay] = jnp.sum(cx[...], axis=0)
    share(cy, cy_send, cy_recv, ay, 16, place_y)
    await_shares(hx, hx_send, hx_recv, ax, 8)
    hy[ay] = jnp.sum(hx[...], axis=0)
    share(hy, hy_send, hy_recv, ay, 16, place_y)
    await_shares(cy, cy_send, cy_recv, ay, 16)
    cz[band] = jnp.sum(cy[...], axis=0)
    share(cz, cz_send, cz_recv, band, BANDS, place_z)
    await_shares(hy, hy_send, hy_recv, ay, 16)
    hz[band] = jnp.sum(hy[...], axis=0)
    share(hz, hz_send, hz_recv, band, BANDS, place_z)
    await_shares(cz, cz_send, cz_recv, band, BANDS)
    corr = square(jnp.concatenate([cz[b] for b in range(BANDS)], axis=0))

    norm2 = jnp.sum(jnp.sum(corr * corr, axis=1, keepdims=True), axis=0, keepdims=True) * 0.125
    norm = jnp.sqrt(norm2)
    identity = jnp.where(iota((16, 128), 0) == iota((16, 128), 1) % 16, 1.0, 0.0).astype(F32)

    def sweep(_, pair):
        iterate, inverse = pair
        middle = 1.5 * identity - 0.5 * small_dot(inverse, iterate)
        return small_dot(iterate, middle), small_dot(middle, inverse)

    _, inverse = lax.fori_loop(0, NS_ITERS, sweep, (corr / norm, identity))
    coeffs = inverse / jnp.sqrt(norm)

    columns = []
    for o in range(2):
        chosen = iota((16, 128), 1) == 2 * band + o
        column = jnp.sum(jnp.where(chosen, coeffs, 0.0), axis=1, keepdims=True)
        columns.append(jnp.broadcast_to(column, (16, 128)))
    upper = iota((8, 128), 0) < 4

    def row(o, j):
        return jnp.broadcast_to(columns[o][j : j + 1], (8, 128))

    for b in range(1, BANDS):
        @pl.when(b > band)
        def _(b=b):
            await_copy(later.at[b], later.at[b], g_send.at[b], g_recv.at[b])

    rotated = jnp.zeros((8, 8, 128), F32)
    for b in range(BANDS):
        block = earlier[b] + later[b]
        straight = jnp.where(upper, row(0, 2 * b), row(1, 2 * b + 1))
        crossed = jnp.where(upper, row(0, 2 * b + 1), row(1, 2 * b))
        rotated = rotated + straight[None] * block + crossed[None] * roll(block, 4, 1)
    rot_out[0] = rotated[:, 0:4, :]
    rot_out[1] = rotated[:, 4:8, :]

    for copy in started[:-7]:
        copy.wait_send()
    for b in range(BANDS):
        @pl.when(b != band)
        def _(b=b):
            band_copy(b, earlier).wait_send()

    await_shares(hz, hz_send, hz_recv, band, BANDS)
    hmat = square(jnp.concatenate([hz[b] for b in range(BANDS)], axis=0))
    prj_out[...] = small_dot(small_dot(coeffs, hmat), coeffs)[:, 0:16]

    for copy in started[-7:]:
        copy.wait_send()


def local(orbitals, potential, support, proj, offsets, coupling):
    dma = pltpu.SemaphoreType.DMA
    vmem = pl.BlockSpec(memory_space=pltpu.VMEM)
    hbm = pl.BlockSpec(memory_space=pltpu.HBM)
    block = (8, 8, 128)
    scratch = [
        pltpu.VMEM((2, 8, 4, 128), F32),
        pltpu.VMEM((8, 4, 128), F32),
        pltpu.VMEM((1, SUPP), jnp.int32),
        pltpu.VMEM((PBLK, SUPP), F32),
        pltpu.SMEM((DOMS,), jnp.int32),
        pltpu.SMEM((NPROJ,), F32),
        dma((6,)),
        pltpu.VMEM((ROUNDS,) + block, F32),
        pltpu.VMEM((PBLK,) + block, F32),
        pltpu.VMEM((640, 128), BF16),
        *[pltpu.VMEM((ROUNDS, 4, 8, 128), F32)] * 2,
        *[pltpu.VMEM((ROUNDS, 2, 8, 128), F32)] * 2,
        *[pltpu.VMEM((ROUNDS, 6, 8, 128), F32)] * 2,
        *[pltpu.VMEM((ROUNDS, 4, 8, 128), F32)] * 2,
        *[pltpu.VMEM((ROUNDS, 2, 8, 128), F32)] * 2,
        pltpu.VMEM((ROUNDS, 5, 1, 128), F32),
        *[pltpu.VMEM((BANDS,) + block, F32)] * 2,
        *[pltpu.VMEM((n, 1, 128), F32) for n in (8, 16, 8)] * 2,
        *[dma((ROUNDS, 6))] * 2,
        *[dma((ROUNDS, 5))] * 2,
        *[dma((BANDS,))] * 2,
        *[dma((n,)) for n in (8, 8, 16, 16, 8, 8)] * 2,
        pltpu.SemaphoreType.REGULAR,
    ]
    rotated, projected = pl.pallas_call(
        kernel,
        out_shape=(
            jax.ShapeDtypeStruct((2, 8, 4, 128), F32),
            jax.ShapeDtypeStruct((16, 16), F32),
        ),
        in_specs=[hbm] * 6,
        out_specs=(vmem, vmem),
        scratch_shapes=scratch,
        compiler_params=pltpu.CompilerParams(
            collective_id=0, has_side_effects=True, vmem_limit_bytes=16 * 1024 * 1024
        ),
    )(
        *[
            pltpu.with_memory_space_constraint(operand, pltpu.HBM)
            for operand in (
                orbitals.reshape(2, 8, 4, 128),
                potential.reshape(8, 4, 128),
                support.reshape(1, SUPP),
                proj,
                offsets,
                coupling,
            )
        ]
    )
    return rotated.reshape(orbitals.shape), projected


def solution(mesh):
    return jax.shard_map(
        local,
        mesh=mesh,
        in_specs=(P("band", "dom", None), P("dom", None), P("dom"), P(None, "dom"), P(), P()),
        out_specs=(P("band", "dom", None), P()),
        check_vma=False,
    )
```

```python
import functools

import jax
import jax.numpy as jnp
from jax import lax
from jax.experimental import pallas as pl
from jax.experimental.pallas import tpu as pltpu
from jax.sharding import PartitionSpec as P

DEG = 4
ROUNDS = DEG + 1
NS_ITERS = 10
NPROJ = 1024
PBLK = 16
SUPP = 512
DOMS = 128
BANDS = 8

STENCIL = [
    -5369.0 / 1800.0,
    12.0 / 7.0,
    -15.0 / 56.0,
    10.0 / 189.0,
    -1.0 / 112.0,
    2.0 / 1925.0,
    -1.0 / 16632.0,
]
HALF = [-0.5 * c for c in STENCIL]
CENTER = 10.0
HALF_WIDTH = 6.0
F32 = jnp.float32
BF16 = jnp.bfloat16
NT = (((1,), (1,)), ((), ()))


def roll(v, shift, axis):
    return pltpu.roll(v, shift % v.shape[axis], axis)


def iota(shape, axis):
    return lax.broadcasted_iota(jnp.int32, shape, axis)


def split3(v):
    high = v.astype(BF16)
    rest = v - high.astype(F32)
    mid = rest.astype(BF16)
    low = (rest - mid.astype(F32)).astype(BF16)
    return high, mid, low


def small_dot(a, b, order=range(16)):
    terms = [
        jnp.broadcast_to(a[:, col : col + 1], (16, 128)) * jnp.broadcast_to(b[r : r + 1, :], (16, 128))
        for r, col in enumerate(order)
    ]
    while len(terms) > 1:
        terms = [x + y for x, y in zip(terms[::2], terms[1::2])]
    return terms[0]


def lane_z(shape):
    return iota(shape, len(shape) - 1) % 32


def lane_y(shape):
    return iota(shape, len(shape) - 1) // 32


def row_y(shape):
    return iota(shape, len(shape) - 2) % 4


def pack_y(v):
    pairs = v.reshape(4, 2, 8, 128)
    even, odd = pairs[:, 0], pairs[:, 1]
    yhi = row_y(even.shape)
    swapped = roll(even, 4, 1)
    first = jnp.where(yhi < 2, swapped, roll(odd, 6, 1))
    last = jnp.where(yhi >= 2, swapped, roll(odd, 2, 1))
    return first, last


def unpack_y(first, last):
    below = jnp.stack([last, roll(last, 2, 1)], axis=1).reshape(8, 8, 128)
    above = jnp.stack([first, roll(first, 6, 1)], axis=1).reshape(8, 8, 128)
    return below, above


def pack_z(v):
    quads = v.reshape(2, 4, 8, 128)
    z = lane_z((2, 8, 128))
    first, last = quads[:, 0], roll(quads[:, 0], 104, 2)
    for i in range(1, 4):
        inside = (z >= 8 * i) & (z < 8 * i + 8)
        first = jnp.where(inside, roll(quads[:, i], 8 * i, 2), first)
        last = jnp.where(inside, roll(quads[:, i], 104 + 8 * i, 2), last)
    return first, last


def unpack_z(first, last):
    above = jnp.stack([roll(first, 32 - 8 * i, 2) for i in range(4)], axis=1)
    below = jnp.stack([roll(last, 120 - 8 * i, 2) for i in range(4)], axis=1)
    return below.reshape(8, 8, 128), above.reshape(8, 8, 128)


def sum_x(v, below, above):
    ext = jnp.concatenate([below, v, above], axis=0)
    total = HALF[1] * (ext[7:15] + ext[5:13])
    for k in range(2, 7):
        total = total + HALF[k] * (ext[6 + k : 14 + k] + ext[6 - k : 14 - k])
    return total


def sum_y(v, below, above):
    yhi = row_y(v.shape)
    up1 = roll(jnp.where(yhi < 1, above, v), 7, 1)
    up2 = roll(jnp.where(yhi < 2, above, v), 6, 1)
    dn1 = roll(jnp.where(yhi >= 3, below, v), 1, 1)
    dn2 = roll(jnp.where(yhi >= 2, below, v), 2, 1)
    p = lane_y((1, 8, 128))
    h = HALF

    def pick(edge, upper, lower):
        return jnp.where(p >= edge, jnp.float32(upper), jnp.float32(lower))

    one = (
        pick(1, h[1], h[3]) * v
        + pick(1, h[5], h[1]) * up1
        + pick(1, 0.0, h[5]) * up2
        + pick(1, h[3], 0.0) * dn1
    )
    two = (
        h[2] * v
        + pick(2, h[6], h[2]) * up1
        + pick(2, 0.0, h[6]) * up2
        + pick(2, h[2], h[6]) * dn1
        + pick(2, h[6], 0.0) * dn2
    )
    three = (
        pick(3, h[3], h[1]) * v
        + pick(3, 0.0, h[3]) * up1
        + pick(3, h[1], h[5]) * dn1
        + pick(3, h[5], 0.0) * dn2
    )
    return h[4] * (up1 + dn1) + roll(one, 96, 2) + roll(two, 64, 2) + roll(three, 32, 2)


def sum_z(v, below, above):
    z = lane_z(v.shape)
    total = None
    for k in range(1, 7):
        up = roll(jnp.where(z < k, above, v), 128 - k, 2)
        down = roll(jnp.where(z >= 32 - k, below, v), k, 2)
        term = HALF[k] * (up + down)
        total = term if total is None else total + term
    return total


def spread_projectors(support, proj):
    high_bits = support // 128
    low_bits = support % 128
    rows = (iota((32, SUPP), 0) == high_bits).astype(F32)
    lanes = (iota((128, SUPP), 0) == low_bits).astype(F32).astype(BF16)
    dense = None
    for part in split3(proj):
        left = (part.astype(F32)[:, None, :] * rows[None]).reshape(PBLK * 32, SUPP)
        term = lax.dot_general(left.astype(BF16), lanes, NT, preferred_element_type=F32)
        dense = term if dense is None else dense + term
    dense = dense.reshape(PBLK * 4, 8, 128)
    turned = roll(dense, 4, 1)
    upper = iota(dense.shape, 1) < 4
    even = jnp.where(upper, dense, turned)
    odd = jnp.where(upper, turned, dense)
    return jnp.stack([even, odd], axis=1).reshape(PBLK, 8, 8, 128)


def lane_sums(rows):
    parts = jnp.concatenate(split3(rows), axis=1)
    return lax.dot_general(jnp.ones((8, 384), BF16), parts, NT, preferred_element_type=F32)[0:1]


def square(rows):
    lane, line = iota((16, 128), 1), iota((16, 128), 0)
    spread = jnp.concatenate([jnp.broadcast_to(rows[z : z + 1], (2, 128)) for z in range(BANDS)], axis=0)
    spread = jnp.where((lane // 8) % 2 == line % 2, spread, 0.0)
    source, target = iota((128, 128), 0), iota((128, 128), 1)
    fold = jnp.where(target % 16 == 2 * (source // 16) + (source // 4) % 2, 1.0, 0.0).astype(BF16)
    parts = jnp.concatenate(split3(spread), axis=0)
    three = jnp.dot(parts, fold, preferred_element_type=F32)
    half = three[0:16] + three[16:32] + three[32:48]
    turned = jnp.concatenate([jnp.transpose(half)[0:16, 0:16]] * 8, axis=1)
    return jnp.where((lane % 16) // 2 <= line // 2, half, turned)


def kernel(
    orb_hbm, pot_hbm, sup_hbm, proj_hbm, off_hbm, coup_hbm, rot_out, prj_out,
    orb, pot, sup, proj, off, coup, load_sem,
    ys, pdense, match, yfirst, ylast, zfirst, zlast,
    xbelow, xabove, ybelow, yabove, zbelow, zabove, inner,
    earlier, later, cx, cy, cz, hx, hy, hz,
    halo_send, halo_recv, inner_send, inner_recv, g_send, g_recv,
    cx_send, cx_recv, cy_send, cy_recv, cz_send, cz_recv,
    hx_send, hx_recv, hy_send, hy_recv, hz_send, hz_recv, later_in,
):
    me = lax.axis_index("dom")
    band = lax.axis_index("band")
    ax, ay = me // 16, me % 16
    by, cz_pos = (me // 4) % 4, me % 4

    def dom_x(i):
        return ((ax + i) % 8) * 16 + ay

    def dom_y(i):
        return ax * 16 + (ay + i) % 16

    x_up, x_down = dom_x(1), dom_x(7)
    y_up = ax * 16 + ((by + 1) % 4) * 4 + cz_pos
    y_down = ax * 16 + ((by + 3) % 4) * 4 + cz_pos
    z_up = me - cz_pos + (cz_pos + 1) % 4
    z_down = me - cz_pos + (cz_pos + 3) % 4
    chain = [((me + step) % DOMS, 2 - step) for step in (-2 + DOMS, -1 + DOMS, 1, 2)]
    chain = [(dom, slot + DOMS if slot < 0 else slot) for dom, slot in chain]

    barrier = pltpu.get_barrier_semaphore()
    near = [(y_up, band), (y_down, band)] + [(dom, band) for dom, _ in chain]
    near += [(x_up, band), (x_down, band), (z_up, band), (z_down, band)]
    for device in near:
        pl.semaphore_signal(barrier, inc=1, device_id=device, device_id_type=pl.DeviceIdType.MESH)
    for b in range(1, BANDS):
        @pl.when(b > band)
        def _(b=b):
            pl.semaphore_signal(barrier, inc=1, device_id=(me, b), device_id_type=pl.DeviceIdType.MESH)

    loads = []
    for i, (src, dst) in enumerate(
        [(orb_hbm, orb), (proj_hbm, proj), (sup_hbm, sup), (off_hbm, off), (pot_hbm, pot), (coup_hbm, coup)]
    ):
        loads.append(pltpu.make_async_copy(src, dst, load_sem.at[i]))
        loads[-1].start()

    started = []

    def send(src, dst, ssem, rsem, dom, to_band):
        copy = pltpu.make_async_remote_copy(
            src_ref=src, dst_ref=dst, send_sem=ssem, recv_sem=rsem,
            device_id=(dom, to_band), device_id_type=pl.DeviceIdType.MESH,
        )
        copy.start()
        started.append(copy)

    def await_copy(src, dst, ssem, rsem):
        pltpu.make_async_remote_copy(
            src_ref=src, dst_ref=dst, send_sem=ssem, recv_sem=rsem,
            device_id=(me, band), device_id_type=pl.DeviceIdType.MESH,
        ).wait_recv()

    def share(buf, ssem, rsem, pos, count, place):
        for i in sorted(range(1, count), key=lambda i: abs(i - count // 2)):
            dom, to_band = place(i)
            send(buf.at[pos], buf.at[pos], ssem.at[i], rsem.at[pos], dom, to_band)

    def await_shares(buf, ssem, rsem, pos, count):
        for i in range(1, count):
            source = (pos + count - i) % count
            await_copy(buf.at[source], buf.at[source], ssem.at[i], rsem.at[source])

    def band_copy(b, buf):
        return pltpu.make_async_remote_copy(
            src_ref=ys.at[DEG], dst_ref=buf.at[band], send_sem=g_send.at[b], recv_sem=g_recv.at[band],
            device_id=(me, b), device_id_type=pl.DeviceIdType.MESH,
        )

    def place_z(i):
        return me, (band + i) % BANDS

    def place_x(i):
        return dom_x(i), band

    def place_y(i):
        return dom_y(i), band

    def pack(k, v):
        yfirst[k], ylast[k] = pack_y(v)
        zfirst[k], zlast[k] = pack_z(v)

    def send_far(k):
        block = ys.at[k]
        hs, hr = halo_send.at[k], halo_recv.at[k]
        send(yfirst.at[k], yabove.at[k], hs.at[0], hr.at[0], y_down, band)
        send(ylast.at[k], ybelow.at[k], hs.at[1], hr.at[1], y_up, band)
        send(block.at[pl.ds(0, 6)], xabove.at[k], hs.at[2], hr.at[2], x_down, band)
        send(block.at[pl.ds(2, 6)], xbelow.at[k], hs.at[3], hr.at[3], x_up, band)

    def send_near(k):
        hs, hr = halo_send.at[k], halo_recv.at[k]
        send(zfirst.at[k], zabove.at[k], hs.at[4], hr.at[4], z_down, band)
        send(zlast.at[k], zbelow.at[k], hs.at[5], hr.at[5], z_up, band)

    def project(k, v):
        inner[k, 2] = lane_sums(
            jnp.concatenate([jnp.sum(pdense[j] * v, axis=0) for j in range(PBLK)], axis=0)
        )

    def send_inner(k):
        for i, (dom, slot) in enumerate(chain):
            send(inner.at[k, 2], inner.at[k, slot], inner_send.at[k, i], inner_recv.at[k, slot], dom, band)

    def exchange(k, v):
        project(k, v)
        send_inner(k)
        pack(k, v)
        send_far(k)
        send_near(k)

    def apply_h(k, v, own, couple):
        hs, hr = halo_send.at[k], halo_recv.at[k]
        await_copy(zabove.at[k], zabove.at[k], hs.at[4], hr.at[4])
        await_copy(zbelow.at[k], zbelow.at[k], hs.at[5], hr.at[5])
        field = own * v + sum_z(v, *unpack_z(zabove[k], zbelow[k]))
        await_copy(xabove.at[k], xabove.at[k], hs.at[2], hr.at[2])
        await_copy(xbelow.at[k], xbelow.at[k], hs.at[3], hr.at[3])
        field = field + sum_x(v, xbelow[k], xabove[k])
        for i, (_, slot) in enumerate(chain):
            slot = 4 - slot
            await_copy(inner.at[k, slot], inner.at[k, slot], inner_send.at[k, i], inner_recv.at[k, slot])
        rows = jnp.concatenate([inner[k, slot] for slot in range(5)], axis=1)
        mine = (iota((8, 640), 1) // 4) % 2 == iota((8, 640), 0) // 4
        rows = jnp.where(mine, jnp.broadcast_to(rows, (8, 640)), 0.0)
        parts = [part.astype(F32) for part in split3(rows)]
        stacked = jnp.concatenate(parts + [jnp.zeros((8, 640), F32)], axis=0).astype(BF16)
        totals = jnp.dot(stacked, match[...], preferred_element_type=F32)
        coefs = (totals[0:8] + totals[8:16] + totals[16:24]) * couple
        for j in range(PBLK):
            field = field + jnp.broadcast_to(coefs[:, j : j + 1], (8, 128))[None] * pdense[j]
        await_copy(yabove.at[k], yabove.at[k], hs.at[0], hr.at[0])
        await_copy(ybelow.at[k], ybelow.at[k], hs.at[1], hr.at[1])
        field = field + sum_y(v, *unpack_y(yabove[k], ybelow[k]))
        return field

    for load in loads:
        load.wait()
    ys[0, :, 0:4, :] = orb[0]
    ys[0, :, 4:8, :] = orb[1]
    current = ys[0]
    pack(0, current)
    pdense[...] = spread_projectors(sup[...], proj[...])
    project(0, current)
    for b in range(BANDS):
        @pl.when(b > band)
        def _(b=b):
            earlier[b] = jnp.zeros((8, 8, 128), F32)

        @pl.when(b <= band)
        def _(b=b):
            later[b] = jnp.zeros((8, 8, 128), F32)

    pl.semaphore_wait(barrier, len(near) + band)
    send_far(0)
    send_inner(0)
    send_near(0)
    for b in range(BANDS - 1):
        @pl.when(b < band)
        def _(b=b):
            pl.semaphore_signal(later_in, inc=1, device_id=(me, b), device_id_type=pl.DeviceIdType.MESH)

    pots = jnp.concatenate([pot[...], pot[...]], axis=1)
    own = pots + jnp.float32(3.0 * HALF[0])
    first_id = off[me]
    couple = jnp.zeros((1, 128), F32)
    lane = iota((1, 128), 1)
    for j in range(PBLK):
        couple = jnp.where(lane == j, coup[(first_id + j) % NPROJ], couple)
    wanted = (first_id + iota((128, 128), 1)) % NPROJ
    for slot in range(5):
        theirs = off[(me + slot - 2 + DOMS) % DOMS]
        have = (theirs + iota((128, 128), 0) // 8) % NPROJ
        match[slot * 128 : slot * 128 + 128, :] = jnp.where(have == wanted, 1.0, 0.0).astype(BF16)

    previous = current
    current = (apply_h(0, current, own, couple) - CENTER * current) * (1.0 / HALF_WIDTH)
    for k in range(1, DEG):
        ys[k] = current
        exchange(k, current)
        following = (apply_h(k, current, own, couple) - CENTER * current) * (2.0 / HALF_WIDTH) - previous
        previous, current = current, following
    ys[DEG] = current

    @pl.when(band < BANDS - 1)
    def _():
        pl.semaphore_wait(later_in, BANDS - 1 - band)

    earlier[band] = current
    exchange(DEG, current)
    for b in reversed(range(BANDS)):
        @pl.when(b > band)
        def _(b=b):
            band_copy(b, earlier).start()

    def columns_of(v):
        upper = iota(v.shape, 1) < 4
        other = roll(v, 4, 1)
        both = [jnp.where(upper, v, other), jnp.where(upper, other, v)]
        return lane_sums(
            jnp.concatenate([jnp.sum(earlier[b] * both[o], axis=0) for b in range(BANDS) for o in range(2)], axis=0)
        )

    for b in range(BANDS - 1):
        @pl.when(b < band)
        def _(b=b):
            await_copy(earlier.at[b], earlier.at[b], g_send.at[b], g_recv.at[b])

    cx[ax] = columns_of(current)
    share(cx, cx_send, cx_recv, ax, 8, place_x)
    hfield = apply_h(DEG, current, own, couple)
    hx[ax] = columns_of(hfield)
    share(hx, hx_send, hx_recv, ax, 8, place_x)
    for b in range(BANDS - 1):
        @pl.when(b < band)
        def _(b=b):
            band_copy(b, later).start()

    await_shares(cx, cx_send, cx_recv, ax, 8)
    cy[ay] = jnp.sum(cx[...], axis=0)
    share(cy, cy_send, cy_recv, ay, 16, place_y)
    await_shares(hx, hx_send, hx_recv, ax, 8)
    hy[ay] = jnp.sum(hx[...], axis=0)
    share(hy, hy_send, hy_recv, ay, 16, place_y)
    await_shares(cy, cy_send, cy_recv, ay, 16)
    cz[band] = jnp.sum(cy[...], axis=0)
    share(cz, cz_send, cz_recv, band, BANDS, place_z)
    await_shares(hy, hy_send, hy_recv, ay, 16)
    hz[band] = jnp.sum(hy[...], axis=0)
    share(hz, hz_send, hz_recv, band, BANDS, place_z)
    await_shares(cz, cz_send, cz_recv, band, BANDS)
    corr = square(jnp.concatenate([cz[b] for b in range(BANDS)], axis=0))

    norm2 = jnp.sum(jnp.sum(corr * corr, axis=1, keepdims=True), axis=0, keepdims=True) * 0.125
    norm = jnp.sqrt(norm2)
    identity = jnp.where(iota((16, 128), 0) == iota((16, 128), 1) % 16, 1.0, 0.0).astype(F32)

    def sweep(_, pair):
        iterate, inverse = pair
        middle = 1.5 * identity - 0.5 * small_dot(inverse, iterate)
        return small_dot(iterate, middle), small_dot(middle, inverse)

    _, inverse = lax.fori_loop(0, NS_ITERS, sweep, (corr / norm, identity))
    coeffs = inverse / jnp.sqrt(norm)

    columns = []
    for o in range(2):
        chosen = iota((16, 128), 1) == 2 * band + o
        column = jnp.sum(jnp.where(chosen, coeffs, 0.0), axis=1, keepdims=True)
        columns.append(jnp.broadcast_to(column, (16, 128)))
    upper = iota((8, 128), 0) < 4

    def row(o, j):
        return jnp.broadcast_to(columns[o][j : j + 1], (8, 128))

    for b in range(1, BANDS):
        @pl.when(b > band)
        def _(b=b):
            await_copy(later.at[b], later.at[b], g_send.at[b], g_recv.at[b])

    rotated = jnp.zeros((8, 8, 128), F32)
    for b in range(BANDS):
        block = earlier[b] + later[b]
        straight = jnp.where(upper, row(0, 2 * b), row(1, 2 * b + 1))
        crossed = jnp.where(upper, row(0, 2 * b + 1), row(1, 2 * b))
        rotated = rotated + straight[None] * block + crossed[None] * roll(block, 4, 1)
    rot_out[0] = rotated[:, 0:4, :]
    rot_out[1] = rotated[:, 4:8, :]

    for copy in started[:-7]:
        copy.wait_send()
    for b in range(BANDS):
        @pl.when(b != band)
        def _(b=b):
            band_copy(b, earlier).wait_send()

    await_shares(hz, hz_send, hz_recv, band, BANDS)
    hmat = square(jnp.concatenate([hz[b] for b in range(BANDS)], axis=0))
    prj_out[...] = small_dot(small_dot(coeffs, hmat), coeffs)[:, 0:16]

    for copy in started[-7:]:
        copy.wait_send()


def local(orbitals, potential, support, proj, offsets, coupling):
    dma = pltpu.SemaphoreType.DMA
    vmem = pl.BlockSpec(memory_space=pltpu.VMEM)
    hbm = pl.BlockSpec(memory_space=pltpu.HBM)
    block = (8, 8, 128)
    scratch = [
        pltpu.VMEM((2, 8, 4, 128), F32),
        pltpu.VMEM((8, 4, 128), F32),
        pltpu.VMEM((1, SUPP), jnp.int32),
        pltpu.VMEM((PBLK, SUPP), F32),
        pltpu.SMEM((DOMS,), jnp.int32),
        pltpu.SMEM((NPROJ,), F32),
        dma((6,)),
        pltpu.VMEM((ROUNDS,) + block, F32),
        pltpu.VMEM((PBLK,) + block, F32),
        pltpu.VMEM((640, 128), BF16),
        *[pltpu.VMEM((ROUNDS, 4, 8, 128), F32)] * 2,
        *[pltpu.VMEM((ROUNDS, 2, 8, 128), F32)] * 2,
        *[pltpu.VMEM((ROUNDS, 6, 8, 128), F32)] * 2,
        *[pltpu.VMEM((ROUNDS, 4, 8, 128), F32)] * 2,
        *[pltpu.VMEM((ROUNDS, 2, 8, 128), F32)] * 2,
        pltpu.VMEM((ROUNDS, 5, 1, 128), F32),
        *[pltpu.VMEM((BANDS,) + block, F32)] * 2,
        *[pltpu.VMEM((n, 1, 128), F32) for n in (8, 16, 8)] * 2,
        *[dma((ROUNDS, 6))] * 2,
        *[dma((ROUNDS, 5))] * 2,
        *[dma((BANDS,))] * 2,
        *[dma((n,)) for n in (8, 8, 16, 16, 8, 8)] * 2,
        pltpu.SemaphoreType.REGULAR,
    ]
    rotated, projected = pl.pallas_call(
        kernel,
        out_shape=(
            jax.ShapeDtypeStruct((2, 8, 4, 128), F32),
            jax.ShapeDtypeStruct((16, 16), F32),
        ),
        in_specs=[hbm] * 6,
        out_specs=(vmem, vmem),
        scratch_shapes=scratch,
        compiler_params=pltpu.CompilerParams(
            collective_id=0, has_side_effects=True, vmem_limit_bytes=16 * 1024 * 1024
        ),
    )(
        *[
            pltpu.with_memory_space_constraint(operand, pltpu.HBM)
            for operand in (
                orbitals.reshape(2, 8, 4, 128),
                potential.reshape(8, 4, 128),
                support.reshape(1, SUPP),
                proj,
                offsets,
                coupling,
            )
        ]
    )
    return rotated.reshape(orbitals.shape), projected


def solution(mesh):
    return jax.shard_map(
        local,
        mesh=mesh,
        in_specs=(P("band", "dom", None), P("dom", None), P("dom"), P(None, "dom"), P(), P()),
        out_specs=(P("band", "dom", None), P()),
        check_vma=False,
    )
```

```python
import functools

import jax
import jax.numpy as jnp
from jax import lax
from jax.experimental import pallas as pl
from jax.experimental.pallas import tpu as pltpu
from jax.sharding import PartitionSpec as P

DEG = 4
ROUNDS = DEG + 1
NS_ITERS = 10
NPROJ = 1024
PBLK = 16
SUPP = 512
DOMS = 128
BANDS = 8

STENCIL = [
    -5369.0 / 1800.0,
    12.0 / 7.0,
    -15.0 / 56.0,
    10.0 / 189.0,
    -1.0 / 112.0,
    2.0 / 1925.0,
    -1.0 / 16632.0,
]
HALF = [-0.5 * c for c in STENCIL]
CENTER = 10.0
HALF_WIDTH = 6.0
F32 = jnp.float32
BF16 = jnp.bfloat16
NT = (((1,), (1,)), ((), ()))


def roll(v, shift, axis):
    return pltpu.roll(v, shift % v.shape[axis], axis)


def iota(shape, axis):
    return lax.broadcasted_iota(jnp.int32, shape, axis)


def split3(v):
    high = v.astype(BF16)
    rest = v - high.astype(F32)
    mid = rest.astype(BF16)
    low = (rest - mid.astype(F32)).astype(BF16)
    return high, mid, low


def small_dot(a, b, order=range(16)):
    terms = [
        jnp.broadcast_to(a[:, col : col + 1], (16, 128)) * jnp.broadcast_to(b[r : r + 1, :], (16, 128))
        for r, col in enumerate(order)
    ]
    while len(terms) > 1:
        terms = [x + y for x, y in zip(terms[::2], terms[1::2])]
    return terms[0]


def lane_z(shape):
    return iota(shape, len(shape) - 1) % 32


def lane_y(shape):
    return iota(shape, len(shape) - 1) // 32


def row_y(shape):
    return iota(shape, len(shape) - 2) % 4


def pack_y(v):
    pairs = v.reshape(4, 2, 8, 128)
    even, odd = pairs[:, 0], pairs[:, 1]
    yhi = row_y(even.shape)
    swapped = roll(even, 4, 1)
    first = jnp.where(yhi < 2, swapped, roll(odd, 6, 1))
    last = jnp.where(yhi >= 2, swapped, roll(odd, 2, 1))
    return first, last


def unpack_y(first, last):
    below = jnp.stack([last, roll(last, 2, 1)], axis=1).reshape(8, 8, 128)
    above = jnp.stack([first, roll(first, 6, 1)], axis=1).reshape(8, 8, 128)
    return below, above


def pack_z(v):
    quads = v.reshape(2, 4, 8, 128)
    z = lane_z((2, 8, 128))
    first, last = quads[:, 0], roll(quads[:, 0], 104, 2)
    for i in range(1, 4):
        inside = (z >= 8 * i) & (z < 8 * i + 8)
        first = jnp.where(inside, roll(quads[:, i], 8 * i, 2), first)
        last = jnp.where(inside, roll(quads[:, i], 104 + 8 * i, 2), last)
    return first, last


def unpack_z(first, last):
    above = jnp.stack([roll(first, 32 - 8 * i, 2) for i in range(4)], axis=1)
    below = jnp.stack([roll(last, 120 - 8 * i, 2) for i in range(4)], axis=1)
    return below.reshape(8, 8, 128), above.reshape(8, 8, 128)


def sum_x(v, below, above):
    ext = jnp.concatenate([below, v, above], axis=0)
    total = HALF[1] * (ext[7:15] + ext[5:13])
    for k in range(2, 7):
        total = total + HALF[k] * (ext[6 + k : 14 + k] + ext[6 - k : 14 - k])
    return total


def sum_y(v, below, above):
    yhi = row_y(v.shape)
    up1 = roll(jnp.where(yhi < 1, above, v), 7, 1)
    up2 = roll(jnp.where(yhi < 2, above, v), 6, 1)
    dn1 = roll(jnp.where(yhi >= 3, below, v), 1, 1)
    dn2 = roll(jnp.where(yhi >= 2, below, v), 2, 1)
    p = lane_y((1, 8, 128))
    h = HALF

    def pick(edge, upper, lower):
        return jnp.where(p >= edge, jnp.float32(upper), jnp.float32(lower))

    one = (
        pick(1, h[1], h[3]) * v
        + pick(1, h[5], h[1]) * up1
        + pick(1, 0.0, h[5]) * up2
        + pick(1, h[3], 0.0) * dn1
    )
    two = (
        h[2] * v
        + pick(2, h[6], h[2]) * up1
        + pick(2, 0.0, h[6]) * up2
        + pick(2, h[2], h[6]) * dn1
        + pick(2, h[6], 0.0) * dn2
    )
    three = (
        pick(3, h[3], h[1]) * v
        + pick(3, 0.0, h[3]) * up1
        + pick(3, h[1], h[5]) * dn1
        + pick(3, h[5], 0.0) * dn2
    )
    return h[4] * (up1 + dn1) + roll(one, 96, 2) + roll(two, 64, 2) + roll(three, 32, 2)


def sum_z(v, below, above):
    z = lane_z(v.shape)
    total = None
    for k in range(1, 7):
        up = roll(jnp.where(z < k, above, v), 128 - k, 2)
        down = roll(jnp.where(z >= 32 - k, below, v), k, 2)
        term = HALF[k] * (up + down)
        total = term if total is None else total + term
    return total


def spread_projectors(support, proj):
    high_bits = support // 128
    low_bits = support % 128
    rows = (iota((32, SUPP), 0) == high_bits).astype(F32)
    lanes = (iota((128, SUPP), 0) == low_bits).astype(F32).astype(BF16)
    dense = None
    for part in split3(proj):
        left = (part.astype(F32)[:, None, :] * rows[None]).reshape(PBLK * 32, SUPP)
        term = lax.dot_general(left.astype(BF16), lanes, NT, preferred_element_type=F32)
        dense = term if dense is None else dense + term
    dense = dense.reshape(PBLK * 4, 8, 128)
    turned = roll(dense, 4, 1)
    upper = iota(dense.shape, 1) < 4
    even = jnp.where(upper, dense, turned)
    odd = jnp.where(upper, turned, dense)
    return jnp.stack([even, odd], axis=1).reshape(PBLK, 8, 8, 128)


def lane_sums(rows):
    parts = jnp.concatenate(split3(rows), axis=1)
    return lax.dot_general(jnp.ones((8, 384), BF16), parts, NT, preferred_element_type=F32)[0:1]


def square(rows):
    lane, line = iota((16, 128), 1), iota((16, 128), 0)
    spread = jnp.concatenate([jnp.broadcast_to(rows[z : z + 1], (2, 128)) for z in range(BANDS)], axis=0)
    spread = jnp.where((lane // 8) % 2 == line % 2, spread, 0.0)
    source, target = iota((128, 128), 0), iota((128, 128), 1)
    fold = jnp.where(target % 16 == 2 * (source // 16) + (source // 4) % 2, 1.0, 0.0).astype(BF16)
    parts = jnp.concatenate(split3(spread), axis=0)
    three = jnp.dot(parts, fold, preferred_element_type=F32)
    half = three[0:16] + three[16:32] + three[32:48]
    turned = jnp.concatenate([jnp.transpose(half)[0:16, 0:16]] * 8, axis=1)
    return jnp.where((lane % 16) // 2 <= line // 2, half, turned)


def kernel(
    orb_hbm, pot_hbm, sup_hbm, proj_hbm, off_hbm, coup_hbm, rot_out, prj_out,
    orb, pot, sup, proj, off, coup, load_sem,
    ys, pdense, match, yfirst, ylast, zfirst, zlast,
    xbelow, xabove, ybelow, yabove, zbelow, zabove, inner,
    earlier, later, cx, cy, cz, hx, hy, hz,
    halo_send, halo_recv, inner_send, inner_recv, g_send, g_recv,
    cx_send, cx_recv, cy_send, cy_recv, cz_send, cz_recv,
    hx_send, hx_recv, hy_send, hy_recv, hz_send, hz_recv, later_in,
):
    me = lax.axis_index("dom")
    band = lax.axis_index("band")
    ax, ay = me // 16, me % 16
    by, cz_pos = (me // 4) % 4, me % 4

    def dom_x(i):
        return ((ax + i) % 8) * 16 + ay

    def dom_y(i):
        return ax * 16 + (ay + i) % 16

    x_up, x_down = dom_x(1), dom_x(7)
    y_up = ax * 16 + ((by + 1) % 4) * 4 + cz_pos
    y_down = ax * 16 + ((by + 3) % 4) * 4 + cz_pos
    z_up = me - cz_pos + (cz_pos + 1) % 4
    z_down = me - cz_pos + (cz_pos + 3) % 4
    chain = [((me + step) % DOMS, 2 - step) for step in (-2 + DOMS, -1 + DOMS, 1, 2)]
    chain = [(dom, slot + DOMS if slot < 0 else slot) for dom, slot in chain]

    barrier = pltpu.get_barrier_semaphore()
    near = [(y_up, band), (y_down, band)] + [(dom, band) for dom, _ in chain]
    near += [(x_up, band), (x_down, band), (z_up, band), (z_down, band)]
    for device in near:
        pl.semaphore_signal(barrier, inc=1, device_id=device, device_id_type=pl.DeviceIdType.MESH)
    for b in range(1, BANDS):
        @pl.when(b > band)
        def _(b=b):
            pl.semaphore_signal(barrier, inc=1, device_id=(me, b), device_id_type=pl.DeviceIdType.MESH)

    loads = []
    for i, (src, dst) in enumerate(
        [(orb_hbm, orb), (proj_hbm, proj), (sup_hbm, sup), (off_hbm, off), (pot_hbm, pot), (coup_hbm, coup)]
    ):
        loads.append(pltpu.make_async_copy(src, dst, load_sem.at[i]))
        loads[-1].start()

    started = []

    def send(src, dst, ssem, rsem, dom, to_band):
        copy = pltpu.make_async_remote_copy(
            src_ref=src, dst_ref=dst, send_sem=ssem, recv_sem=rsem,
            device_id=(dom, to_band), device_id_type=pl.DeviceIdType.MESH,
        )
        copy.start()
        started.append(copy)

    def await_copy(src, dst, ssem, rsem):
        pltpu.make_async_remote_copy(
            src_ref=src, dst_ref=dst, send_sem=ssem, recv_sem=rsem,
            device_id=(me, band), device_id_type=pl.DeviceIdType.MESH,
        ).wait_recv()

    def share(buf, ssem, rsem, pos, count, place):
        for i in sorted(range(1, count), key=lambda i: abs(i - count // 2)):
            dom, to_band = place(i)
            send(buf.at[pos], buf.at[pos], ssem.at[i], rsem.at[pos], dom, to_band)

    def await_shares(buf, ssem, rsem, pos, count):
        for i in range(1, count):
            source = (pos + count - i) % count
            await_copy(buf.at[source], buf.at[source], ssem.at[i], rsem.at[source])

    def band_copy(b, buf):
        return pltpu.make_async_remote_copy(
            src_ref=ys.at[DEG], dst_ref=buf.at[band], send_sem=g_send.at[b], recv_sem=g_recv.at[band],
            device_id=(me, b), device_id_type=pl.DeviceIdType.MESH,
        )

    def place_z(i):
        return me, (band + i) % BANDS

    def place_x(i):
        return dom_x(i), band

    def place_y(i):
        return dom_y(i), band

    def pack(k, v):
        yfirst[k], ylast[k] = pack_y(v)
        zfirst[k], zlast[k] = pack_z(v)

    def send_far(k):
        block = ys.at[k]
        hs, hr = halo_send.at[k], halo_recv.at[k]
        send(yfirst.at[k], yabove.at[k], hs.at[0], hr.at[0], y_down, band)
        send(ylast.at[k], ybelow.at[k], hs.at[1], hr.at[1], y_up, band)
        send(block.at[pl.ds(0, 6)], xabove.at[k], hs.at[2], hr.at[2], x_down, band)
        send(block.at[pl.ds(2, 6)], xbelow.at[k], hs.at[3], hr.at[3], x_up, band)

    def send_near(k):
        hs, hr = halo_send.at[k], halo_recv.at[k]
        send(zfirst.at[k], zabove.at[k], hs.at[4], hr.at[4], z_down, band)
        send(zlast.at[k], zbelow.at[k], hs.at[5], hr.at[5], z_up, band)

    def project(k, v):
        inner[k, 2] = lane_sums(
            jnp.concatenate([jnp.sum(pdense[j] * v, axis=0) for j in range(PBLK)], axis=0)
        )

    def send_inner(k):
        for i, (dom, slot) in enumerate(chain):
            send(inner.at[k, 2], inner.at[k, slot], inner_send.at[k, i], inner_recv.at[k, slot], dom, band)

    def exchange(k, v):
        project(k, v)
        send_inner(k)
        pack(k, v)
        send_far(k)
        send_near(k)

    def apply_h(k, v, own, couple):
        hs, hr = halo_send.at[k], halo_recv.at[k]
        await_copy(zabove.at[k], zabove.at[k], hs.at[4], hr.at[4])
        await_copy(zbelow.at[k], zbelow.at[k], hs.at[5], hr.at[5])
        field = own * v + sum_z(v, *unpack_z(zabove[k], zbelow[k]))
        await_copy(xabove.at[k], xabove.at[k], hs.at[2], hr.at[2])
        await_copy(xbelow.at[k], xbelow.at[k], hs.at[3], hr.at[3])
        field = field + sum_x(v, xbelow[k], xabove[k])
        for i, (_, slot) in enumerate(chain):
            slot = 4 - slot
            await_copy(inner.at[k, slot], inner.at[k, slot], inner_send.at[k, i], inner_recv.at[k, slot])
        rows = jnp.concatenate([inner[k, slot] for slot in range(5)], axis=1)
        mine = (iota((8, 640), 1) // 4) % 2 == iota((8, 640), 0) // 4
        rows = jnp.where(mine, jnp.broadcast_to(rows, (8, 640)), 0.0)
        parts = [part.astype(F32) for part in split3(rows)]
        stacked = jnp.concatenate(parts + [jnp.zeros((8, 640), F32)], axis=0).astype(BF16)
        totals = jnp.dot(stacked, match[...], preferred_element_type=F32)
        coefs = (totals[0:8] + totals[8:16] + totals[16:24]) * couple
        for j in range(PBLK):
            field = field + jnp.broadcast_to(coefs[:, j : j + 1], (8, 128))[None] * pdense[j]
        await_copy(yabove.at[k], yabove.at[k], hs.at[0], hr.at[0])
        await_copy(ybelow.at[k], ybelow.at[k], hs.at[1], hr.at[1])
        field = field + sum_y(v, *unpack_y(yabove[k], ybelow[k]))
        return field

    for load in loads:
        load.wait()
    ys[0, :, 0:4, :] = orb[0]
    ys[0, :, 4:8, :] = orb[1]
    current = ys[0]
    pack(0, current)
    pdense[...] = spread_projectors(sup[...], proj[...])
    project(0, current)
    for b in range(BANDS):
        @pl.when(b > band)
        def _(b=b):
            earlier[b] = jnp.zeros((8, 8, 128), F32)

        @pl.when(b <= band)
        def _(b=b):
            later[b] = jnp.zeros((8, 8, 128), F32)

    pl.semaphore_wait(barrier, len(near) + band)
    send_far(0)
    send_inner(0)
    send_near(0)
    for b in range(BANDS - 1):
        @pl.when(b < band)
        def _(b=b):
            pl.semaphore_signal(later_in, inc=1, device_id=(me, b), device_id_type=pl.DeviceIdType.MESH)

    pots = jnp.concatenate([pot[...], pot[...]], axis=1)
    own = pots + jnp.float32(3.0 * HALF[0])
    first_id = off[me]
    couple = jnp.zeros((1, 128), F32)
    lane = iota((1, 128), 1)
    for j in range(PBLK):
        couple = jnp.where(lane == j, coup[(first_id + j) % NPROJ], couple)
    wanted = (first_id + iota((128, 128), 1)) % NPROJ
    for slot in range(5):
        theirs = off[(me + slot - 2 + DOMS) % DOMS]
        have = (theirs + iota((128, 128), 0) // 8) % NPROJ
        match[slot * 128 : slot * 128 + 128, :] = jnp.where(have == wanted, 1.0, 0.0).astype(BF16)

    previous = current
    current = (apply_h(0, current, own, couple) - CENTER * current) * (1.0 / HALF_WIDTH)
    for k in range(1, DEG):
        ys[k] = current
        exchange(k, current)
        following = (apply_h(k, current, own, couple) - CENTER * current) * (2.0 / HALF_WIDTH) - previous
        previous, current = current, following
    ys[DEG] = current

    @pl.when(band < BANDS - 1)
    def _():
        pl.semaphore_wait(later_in, BANDS - 1 - band)

    earlier[band] = current
    exchange(DEG, current)
    for b in reversed(range(BANDS)):
        @pl.when(b > band)
        def _(b=b):
            band_copy(b, earlier).start()

    def columns_of(v):
        upper = iota(v.shape, 1) < 4
        other = roll(v, 4, 1)
        both = [jnp.where(upper, v, other), jnp.where(upper, other, v)]
        return lane_sums(
            jnp.concatenate([jnp.sum(earlier[b] * both[o], axis=0) for b in range(BANDS) for o in range(2)], axis=0)
        )

    for b in range(BANDS - 1):
        @pl.when(b < band)
        def _(b=b):
            await_copy(earlier.at[b], earlier.at[b], g_send.at[b], g_recv.at[b])

    cx[ax] = columns_of(current)
    share(cx, cx_send, cx_recv, ax, 8, place_x)
    hfield = apply_h(DEG, current, own, couple)
    hx[ax] = columns_of(hfield)
    share(hx, hx_send, hx_recv, ax, 8, place_x)
    await_shares(cx, cx_send, cx_recv, ax, 8)
    cy[ay] = jnp.sum(cx[...], axis=0)
    share(cy, cy_send, cy_recv, ay, 16, place_y)
    for b in range(BANDS - 1):
        @pl.when(b < band)
        def _(b=b):
            band_copy(b, later).start()

    await_shares(hx, hx_send, hx_recv, ax, 8)
    hy[ay] = jnp.sum(hx[...], axis=0)
    share(hy, hy_send, hy_recv, ay, 16, place_y)
    await_shares(cy, cy_send, cy_recv, ay, 16)
    cz[band] = jnp.sum(cy[...], axis=0)
    share(cz, cz_send, cz_recv, band, BANDS, place_z)
    await_shares(hy, hy_send, hy_recv, ay, 16)
    hz[band] = jnp.sum(hy[...], axis=0)
    share(hz, hz_send, hz_recv, band, BANDS, place_z)
    await_shares(cz, cz_send, cz_recv, band, BANDS)
    corr = square(jnp.concatenate([cz[b] for b in range(BANDS)], axis=0))

    norm2 = jnp.sum(jnp.sum(corr * corr, axis=1, keepdims=True), axis=0, keepdims=True) * 0.125
    norm = jnp.sqrt(norm2)
    identity = jnp.where(iota((16, 128), 0) == iota((16, 128), 1) % 16, 1.0, 0.0).astype(F32)

    def sweep(_, pair):
        iterate, inverse = pair
        middle = 1.5 * identity - 0.5 * small_dot(inverse, iterate)
        return small_dot(iterate, middle), small_dot(middle, inverse)

    _, inverse = lax.fori_loop(0, NS_ITERS, sweep, (corr / norm, identity))
    coeffs = inverse / jnp.sqrt(norm)

    columns = []
    for o in range(2):
        chosen = iota((16, 128), 1) == 2 * band + o
        column = jnp.sum(jnp.where(chosen, coeffs, 0.0), axis=1, keepdims=True)
        columns.append(jnp.broadcast_to(column, (16, 128)))
    upper = iota((8, 128), 0) < 4

    def row(o, j):
        return jnp.broadcast_to(columns[o][j : j + 1], (8, 128))

    for b in range(1, BANDS):
        @pl.when(b > band)
        def _(b=b):
            await_copy(later.at[b], later.at[b], g_send.at[b], g_recv.at[b])

    rotated = jnp.zeros((8, 8, 128), F32)
    for b in range(BANDS):
        block = earlier[b] + later[b]
        straight = jnp.where(upper, row(0, 2 * b), row(1, 2 * b + 1))
        crossed = jnp.where(upper, row(0, 2 * b + 1), row(1, 2 * b))
        rotated = rotated + straight[None] * block + crossed[None] * roll(block, 4, 1)
    rot_out[0] = rotated[:, 0:4, :]
    rot_out[1] = rotated[:, 4:8, :]

    for copy in started[:-7]:
        copy.wait_send()
    for b in range(BANDS):
        @pl.when(b != band)
        def _(b=b):
            band_copy(b, earlier).wait_send()

    await_shares(hz, hz_send, hz_recv, band, BANDS)
    hmat = square(jnp.concatenate([hz[b] for b in range(BANDS)], axis=0))
    prj_out[...] = small_dot(small_dot(coeffs, hmat), coeffs)[:, 0:16]

    for copy in started[-7:]:
        copy.wait_send()


def local(orbitals, potential, support, proj, offsets, coupling):
    dma = pltpu.SemaphoreType.DMA
    vmem = pl.BlockSpec(memory_space=pltpu.VMEM)
    hbm = pl.BlockSpec(memory_space=pltpu.HBM)
    block = (8, 8, 128)
    scratch = [
        pltpu.VMEM((2, 8, 4, 128), F32),
        pltpu.VMEM((8, 4, 128), F32),
        pltpu.VMEM((1, SUPP), jnp.int32),
        pltpu.VMEM((PBLK, SUPP), F32),
        pltpu.SMEM((DOMS,), jnp.int32),
        pltpu.SMEM((NPROJ,), F32),
        dma((6,)),
        pltpu.VMEM((ROUNDS,) + block, F32),
        pltpu.VMEM((PBLK,) + block, F32),
        pltpu.VMEM((640, 128), BF16),
        *[pltpu.VMEM((ROUNDS, 4, 8, 128), F32)] * 2,
        *[pltpu.VMEM((ROUNDS, 2, 8, 128), F32)] * 2,
        *[pltpu.VMEM((ROUNDS, 6, 8, 128), F32)] * 2,
        *[pltpu.VMEM((ROUNDS, 4, 8, 128), F32)] * 2,
        *[pltpu.VMEM((ROUNDS, 2, 8, 128), F32)] * 2,
        pltpu.VMEM((ROUNDS, 5, 1, 128), F32),
        *[pltpu.VMEM((BANDS,) + block, F32)] * 2,
        *[pltpu.VMEM((n, 1, 128), F32) for n in (8, 16, 8)] * 2,
        *[dma((ROUNDS, 6))] * 2,
        *[dma((ROUNDS, 5))] * 2,
        *[dma((BANDS,))] * 2,
        *[dma((n,)) for n in (8, 8, 16, 16, 8, 8)] * 2,
        pltpu.SemaphoreType.REGULAR,
    ]
    rotated, projected = pl.pallas_call(
        kernel,
        out_shape=(
            jax.ShapeDtypeStruct((2, 8, 4, 128), F32),
            jax.ShapeDtypeStruct((16, 16), F32),
        ),
        in_specs=[hbm] * 6,
        out_specs=(vmem, vmem),
        scratch_shapes=scratch,
        compiler_params=pltpu.CompilerParams(
            collective_id=0, has_side_effects=True, vmem_limit_bytes=16 * 1024 * 1024
        ),
    )(
        *[
            pltpu.with_memory_space_constraint(operand, pltpu.HBM)
            for operand in (
                orbitals.reshape(2, 8, 4, 128),
                potential.reshape(8, 4, 128),
                support.reshape(1, SUPP),
                proj,
                offsets,
                coupling,
            )
        ]
    )
    return rotated.reshape(orbitals.shape), projected


def solution(mesh):
    return jax.shard_map(
        local,
        mesh=mesh,
        in_specs=(P("band", "dom", None), P("dom", None), P("dom"), P(None, "dom"), P(), P()),
        out_specs=(P("band", "dom", None), P()),
        check_vma=False,
    )
```
